128 devices in a mesh: row: 8 (over y, core), col: 16 (over x, z).
Axes of the slice: x: 4, y: 4, z: 4, core: 2. Of those that a mesh axis runs over, the one named last changes fastest.
Arguments:
- features: bfloat16 [65536, 64], P(('row', 'col')), may hold values from -12 to 12
- task_id: int32 [65536], P(('row', 'col')), may hold values from 0 to 255
- task_count: int32 [256], replicated, may hold values from 103 to 409, as said below
- task_rank: int32 [65536], P(('row', 'col')), may hold values from 0 to 408, as said below
- probes: bfloat16 [65536, 32], P(('row', 'col')), may hold values from -6 to 6
- net_w: bfloat16 [64, 64], replicated, may hold values from -0.75 to 0.75
- net_b: float32 [64], replicated, may hold values from -3 to 3
- inv_scale: float32 [64], replicated, may hold values from 0.2 to 0.7
- task_mix: float32 [256, 4], replicated, may hold values from -3 to 3
- task_diag: float32 [256], replicated, may hold values from 0.2 to 1
- task_noise: float32 [256], replicated, may hold values from 0.05 to 0.5
Outputs:
- residual: float32 [65536, 32], P(('row', 'col'))
- direction: float32 [65536, 32], P(('row', 'col'))
- step_length: float32 [32], replicated
- update_weight: float32 [32], replicated
The draws below stay inside these ranges and needn't reach their ends.
Inputs may be any that keep to these rules, and one draw needn't show every extreme that they name: Task t holds exactly task_count[t] observations; their task_rank values are 0 to task_count[t] - 1, each once. `task_rank`: every device holds exactly 4 observations whose sorted position falls in each device's block of 512 positions.
All inputs are finite; a program needn't handle non-finite values.
Results may differ from the reference program's by a relative error of at most 0.0044.
The reference program's roundings to bfloat16 on the way (of `latent`, `sorted_z`, `scaled` and `kern`) count: a program that leaves them out, or rounds other values in their place, can miss the bound.
Values may be sent and summed in bfloat16 or wider, within the bound.
No kernel may reach another device: no remote copies, remote signals or barrier semaphores. Data moves between devices by JAX's collectives and lax.ppermute only.
A program may use at most 64 MiB of HBM per device.

```python
import math
import jax
import jax.numpy as jnp
from jax import lax

ROWS_DEV = 512
FEAT = 64
TASKS = 256
RANK = 4
WIDTH = 32
SHARDS = 128
PER = 4
TOKENS = 65536


def layout(key):
    base = TOKENS // TASKS
    reach = 3 * base // 5
    half = TASKS // 2
    key_one, key_two, key_three, key_four = jax.random.split(key, 4)
    shifts = jax.random.randint(key_one, (half,), -reach, reach + 1).astype(jnp.int32)
    shifts = shifts.at[0].set(reach)
    paired = jnp.concatenate([base + shifts, base - shifts]).astype(jnp.int32)
    mixing = jax.random.permutation(key_two, TASKS)
    counts = paired[mixing]
    offsets = jnp.cumsum(counts) - counts
    tasks_sorted = jnp.repeat(jnp.arange(TASKS, dtype=jnp.int32), counts, total_repeat_length=TOKENS)
    places = jnp.arange(TOKENS, dtype=jnp.int32)
    ranks = (places - offsets[tasks_sorted]).astype(jnp.int32)
    target = places // ROWS_DEV
    inner = places % ROWS_DEV
    scores = jax.random.randint(key_three, (SHARDS, ROWS_DEV), 0, 1 << 20) * ROWS_DEV + jnp.arange(ROWS_DEV, dtype=jnp.int32)[None, :]
    shuffle_in = jnp.argsort(scores, axis=1).astype(jnp.int32)
    moved = shuffle_in[target, inner]
    source = (moved // PER + target) % SHARDS
    before = target * PER + moved % PER
    scores_two = jax.random.randint(key_four, (SHARDS, ROWS_DEV), 0, 1 << 20) * ROWS_DEV + jnp.arange(ROWS_DEV, dtype=jnp.int32)[None, :]
    shuffle_out = jnp.argsort(scores_two, axis=1).astype(jnp.int32)
    arrival = source * ROWS_DEV + shuffle_out[source, before]
    task_arrival = jnp.zeros((TOKENS,), jnp.int32).at[arrival].set(tasks_sorted)
    rank_arrival = jnp.zeros((TOKENS,), jnp.int32).at[arrival].set(ranks)
    return (task_arrival, counts, rank_arrival)


def draw_task_id(key, part):
    return layout(key)[0]


def draw_task_count(key, part):
    return layout(key)[1]


def draw_task_rank(key, part):
    return layout(key)[2]


def block_scale(stream_key, dims, cuts, least, high):
    loudness = 1.0
    for dim, shards_of in cuts:
        steps = jax.random.uniform(jax.random.fold_in(jax.random.fold_in(stream_key, 6), dim), (shards_of,), jnp.float32, least / len(cuts), high / len(cuts))
        loudness = loudness * jnp.repeat(jnp.exp(steps), dims[dim] // shards_of).reshape((-1,) + (1,) * (len(dims) - 1 - dim))
    return loudness


def scatter_about(own_key, shape, deviation, bound, shards=(), kind=jnp.bfloat16):
    level = block_scale(own_key, shape, shards, -0.22, 0.18) if shards else 1.0
    values = jax.random.normal(own_key, shape, jnp.float32) * deviation * level
    return jnp.minimum(jnp.maximum(values, -bound), bound).astype(kind)


def setup_inputs(seed: int = 0) -> dict:
    arg_keys = jax.random.split(jax.random.key(seed), 12)
    return {
        "features": scatter_about(arg_keys[0], (TOKENS, FEAT), 2.0, 12.0, ((0, 128),)),
        "task_id": draw_task_id(jax.random.fold_in(arg_keys[11], 71), 0),
        "task_count": draw_task_count(jax.random.fold_in(arg_keys[11], 71), 0),
        "task_rank": draw_task_rank(jax.random.fold_in(arg_keys[11], 71), 0),
        "probes": scatter_about(arg_keys[4], (TOKENS, WIDTH), 1.0, 6.0, ((0, 128),)),
        "net_w": scatter_about(arg_keys[5], (FEAT, FEAT), FEAT ** -0.5, 0.75),
        "net_b": scatter_about(arg_keys[6], (FEAT,), 0.7, 3.0, (), jnp.float32),
        "inv_scale": jnp.clip(jnp.exp(jax.random.uniform(arg_keys[7], (FEAT,), jnp.float32, math.log(0.2), math.log(0.7))), 0.2, 0.7),
        "task_mix": scatter_about(arg_keys[8], (TASKS, RANK), 0.6, 3.0, (), jnp.float32),
        "task_diag": jnp.clip(jnp.exp(jax.random.uniform(arg_keys[9], (TASKS,), jnp.float32, math.log(0.2), math.log(1.0))), 0.2, 1.0),
        "task_noise": jnp.clip(jnp.exp(jax.random.uniform(arg_keys[10], (TASKS,), jnp.float32, math.log(0.05), math.log(0.5))), 0.05, 0.5),
    }


def reference(features, task_id, task_count, task_rank, probes, net_w, net_b, inv_scale, task_mix, task_diag, task_noise):
    offsets = (jnp.cumsum(task_count) - task_count).astype(jnp.int32)
    position = (offsets[task_id] + task_rank).astype(jnp.int32)
    hidden = jnp.tanh(jnp.dot(features, net_w, preferred_element_type=jnp.float32) + net_b)
    latent = (hidden * inv_scale).astype(jnp.bfloat16)
    sorted_z = jnp.zeros_like(latent).at[position].set(latent)
    sorted_v = jnp.zeros_like(probes).at[position].set(probes)
    sorted_t = jnp.zeros((TOKENS,), jnp.int32).at[position].set(task_id)
    weights = task_mix[sorted_t]
    kappa = task_diag[sorted_t]
    noise = task_noise[sorted_t]
    v_float = sorted_v.astype(jnp.float32)
    scaled = (weights[:, :, None] * v_float[:, None, :]).reshape(TOKENS, RANK * WIDTH).astype(jnp.bfloat16)
    norms = jnp.sum(sorted_z.astype(jnp.float32) ** 2, axis=1)
    block = 1024 if TOKENS % 1024 == 0 else TOKENS

    def one_block(pieces):
        zb, nb, tb, wb, kb = pieces
        cross = lax.dot_general(zb, sorted_z, (((1,), (1,)), ((), ())), preferred_element_type=jnp.float32)
        dist = jnp.maximum(nb[:, None] + norms[None, :] - 2.0 * cross, 0.0)
        kern = jnp.exp(-0.5 * dist).astype(jnp.bfloat16)
        prod = jnp.dot(kern, scaled, preferred_element_type=jnp.float32).reshape(block, RANK, WIDTH)
        low = jnp.sum(wb[:, :, None] * prod, axis=1)
        same = jnp.where(tb[:, None] == sorted_t[None, :], kern, jnp.zeros_like(kern))
        diag = jnp.dot(same, sorted_v, preferred_element_type=jnp.float32)
        return low + kb[:, None] * diag

    count = TOKENS // block
    pieces = (sorted_z.reshape(count, block, FEAT), norms.reshape(count, block), sorted_t.reshape(count, block),
              weights.reshape(count, block, RANK), kappa.reshape(count, block))
    image = lax.map(one_block, pieces).reshape(TOKENS, WIDTH) + noise[:, None] * v_float
    start = jnp.sum(v_float * v_float, axis=0)
    curve = jnp.sum(v_float * image, axis=0)
    alpha = start / curve
    residual = v_float - alpha * image
    finish = jnp.sum(residual * residual, axis=0)
    beta = finish / start
    direction = residual + beta * v_float
    return residual, direction, alpha, beta
```

```python
import functools

import jax
import jax.numpy as jnp
from jax import lax
from jax.experimental import pallas as pl
from jax.experimental.pallas import tpu as pltpu
from jax.sharding import PartitionSpec as P

F32 = jnp.float32
BF16 = jnp.bfloat16
VMEM = pl.BlockSpec(memory_space=pltpu.VMEM)
SMEM = pl.BlockSpec(memory_space=pltpu.SMEM)
PARAMS = pltpu.CompilerParams(vmem_limit_bytes=48 * 1024 * 1024)
V0, P0, T0 = 64, 96, 98


def iota(shape, dim):
    return lax.broadcasted_iota(jnp.int32, shape, dim)


def split3(x):
    hi = x.astype(BF16)
    rest = x - hi.astype(F32)
    mid = rest.astype(BF16)
    low = (rest - mid.astype(F32)).astype(BF16)
    return hi, mid, low


def task_starts(counts):
    n = counts.shape[1]
    before = iota((n, n), 1) < iota((n, n), 0)
    start = jnp.sum(jnp.where(before, counts, 0.0), axis=1, keepdims=True)
    own = iota((n, n), 1) == iota((n, n), 0)
    return start, start + jnp.sum(jnp.where(own, counts, 0.0), axis=1, keepdims=True)


def pack_kernel(feat, tid, cnt, rank, probes, net_w, net_b, scale, packed, payload):
    rows = feat.shape[0]
    ntask = cnt.shape[1]
    start, _ = task_starts(cnt[...].astype(F32))
    task = tid[...]
    hit = iota((ntask, rows), 0) == task
    pos = jnp.sum(jnp.where(hit, start, 0.0), axis=0, keepdims=True) + rank[...].astype(F32)
    both = jnp.concatenate([pos, task.astype(F32), jnp.zeros((6, rows), F32)], axis=0).T
    pos_col, task_col = both[:, 0:1], both[:, 1:2]
    order = jnp.sum((pos_col < pos).astype(F32), axis=0, keepdims=True)
    placing = (iota((rows, rows), 0) == order.astype(jnp.int32)).astype(BF16)
    hidden = jnp.tanh(
        jnp.dot(feat[...], net_w[...], preferred_element_type=F32) + net_b[...]
    )
    latent = (hidden * scale[...]).astype(BF16)
    local = pos_col - jnp.floor(pos_col * (1.0 / rows)) * rows
    high = jnp.floor(local * (1.0 / 16.0))
    lane = iota((rows, 128 - P0), 1)
    extra = jnp.where(
        lane == 0,
        high,
        jnp.where(lane == 1, local - 16.0 * high, jnp.where(lane == T0 - P0, task_col, 0.0)),
    )
    whole = jnp.concatenate([latent, probes[...], extra.astype(BF16)], axis=1)
    payload[...] = whole
    packed[...] = jnp.dot(placing, whole, preferred_element_type=F32).astype(BF16)


def rows_kernel(n_col, flat, cnt, table, rows_w, own):
    half = rows_w.shape[2] // n_col
    ntask = cnt.shape[1]
    start, end = task_starts(cnt[...].astype(F32))
    block = own.shape[1]
    group = (flat[0] // n_col) * (n_col * block)
    tab = jnp.concatenate(split3(table[...]), axis=0)

    def look(first, count):
        pos = (first + iota((1, count), 1)).astype(F32)
        hit = jnp.logical_and(start <= pos, pos < end)
        got = jnp.dot(tab, hit.astype(BF16), preferred_element_type=F32)
        return hit, got[0:8] + got[8:16] + got[16:24]

    for c in range(n_col):
        _, got = look(group + c * block, block)
        for h in range(2):
            rows_w[h, :, c * half : (c + 1) * half] = got[:, h * half : (h + 1) * half]
    hit, got = look(flat[0] * block, block)
    low = jnp.sum(jnp.where(hit, start, 0.0), axis=0, keepdims=True)
    high = jnp.sum(jnp.where(hit, end, 0.0), axis=0, keepdims=True)
    own[...] = jnp.concatenate([low, high, got[4:6], jnp.zeros((4, block), F32)], axis=0)


def sort_kernel(got, out_t, za, zb):
    rows = got.shape[0]
    data = got[...]
    place = data[:, P0 : P0 + 1].astype(F32) * 16.0 + data[:, P0 + 1 : P0 + 2].astype(F32)
    onehot = (iota((rows, rows), 1) == place.astype(jnp.int32)).astype(BF16)
    ordered = lax.dot_general(
        data, onehot, (((0,), (0,)), ((), ())), preferred_element_type=F32
    ).astype(BF16)
    out_t[...] = ordered[:P0]
    half = rows // 2
    for c in range(za.shape[0]):
        za[c] = ordered[:V0, :half]
        zb[c] = ordered[:V0, half:]


def cols_kernel(table, *refs):
    chunks, (zc, st) = refs[:-2], refs[-2:]
    rows = chunks[0].shape[0]
    ntask = table.shape[1]
    tab = jnp.concatenate(split3(table[...]), axis=0)
    for k, ref in enumerate(chunks):
        data = ref[...].astype(F32)
        lane = iota((rows, 128), 1)
        z = jnp.where(lane < V0, data, 0.0)
        norm = jnp.sum(z * z, axis=1, keepdims=True) * -0.5
        hi, mid, low = (a.astype(F32) for a in split3(norm))
        z = jnp.where(lane == V0, hi, z)
        z = jnp.where(lane == V0 + 1, mid, z)
        z = jnp.where(lane == V0 + 2, low, z)
        z = jnp.where(jnp.logical_and(lane > V0 + 2, lane < V0 + 6), 1.0, z)
        zc[k * rows : (k + 1) * rows, :] = z.astype(BF16)
        turned = data.T
        task = turned[T0 : T0 + 1].astype(jnp.int32)
        hit = (iota((ntask, rows), 0) == task).astype(BF16)
        got = jnp.dot(tab, hit, preferred_element_type=F32)
        weight = got[0:8] + got[8:16] + got[16:24]
        values = turned[V0:P0]
        width = P0 - V0
        for q in range(4):
            st[q * width : (q + 1) * width, k * rows : (k + 1) * rows] = (
                weight[q : q + 1] * values
            ).astype(BF16)


def augment_rows(z):
    n = z.shape[1]
    zf = z.astype(F32)
    norm = jnp.sum(zf * zf, axis=0, keepdims=True) * -0.5
    hi, mid, low = (a.astype(F32) for a in split3(norm))
    sub = iota((16, n), 0)
    extra = jnp.where(sub < 3, 1.0, 0.0)
    extra = jnp.where(sub == 3, hi, extra)
    extra = jnp.where(sub == 4, mid, extra)
    extra = jnp.where(sub == 5, low, extra)
    return jnp.concatenate([z, extra.astype(BF16), jnp.zeros((48, n), BF16)], axis=0)


def main_kernel(tile, zr, weight, zc, st, out):
    z = augment_rows(jnp.concatenate([zr[c] for c in range(zr.shape[0])], axis=1))
    total = None
    for j in range(zc.shape[0] // tile):
        span = slice(j * tile, (j + 1) * tile)
        x = jnp.dot(zc[span, :], z, preferred_element_type=F32)
        kern = jnp.minimum(jnp.exp(x).astype(BF16), jnp.asarray(1.0, BF16))
        part = jnp.dot(st[:, span], kern, preferred_element_type=F32)
        total = part if total is None else total + part
    width = total.shape[0] // 4
    summed = weight[0:1] * total[:width]
    for q in range(1, 4):
        summed = summed + weight[q : q + 1] * total[q * width : (q + 1) * width]
    half = zr.shape[2]
    for c in range(zr.shape[0]):
        out[c] = summed[:, c * half : (c + 1) * half].astype(out.dtype)


def main_call(zr, weight, zc, st):
    n_col, feat, half = zr.shape
    cols = zc.shape[0]
    step = 4
    width = st.shape[0] // 4
    return pl.pallas_call(
        functools.partial(main_kernel, 1024),
        grid=(n_col // step,),
        in_specs=[
            pl.BlockSpec((step, feat, half), lambda i: (i, 0, 0)),
            pl.BlockSpec((8, step * half), lambda i: (0, i)),
            pl.BlockSpec((cols, 128), lambda i: (0, 0)),
            pl.BlockSpec((st.shape[0], cols), lambda i: (0, 0)),
        ],
        out_specs=pl.BlockSpec((step, width, half), lambda i: (i, 0, 0)),
        out_shape=jax.ShapeDtypeStruct((n_col, width, half), F32),
        compiler_params=PARAMS,
        cost_estimate=pl.CostEstimate(
            flops=2 * n_col * half * cols * 512, bytes_accessed=4 << 20, transcendentals=0
        ),
        name="product",
    )(zr, weight, zc, st)


def same_kernel(flat, own, mid, prev, nxt, out):
    block = own.shape[1]
    z = augment_rows(mid[:V0])
    low, high = own[0:1], own[1:2]
    total = None
    for k, ref in enumerate((prev, mid, nxt)):
        data = ref[...]
        zt = augment_rows(data[:V0])
        zt = jnp.concatenate([zt[:V0], swap_norm(zt[V0 : V0 + 16]), zt[V0 + 16 :]], axis=0)
        x = lax.dot_general(zt, z, (((0,), (0,)), ((), ())), preferred_element_type=F32)
        kern = jnp.minimum(jnp.exp(x).astype(BF16), jnp.asarray(1.0, BF16)).astype(F32)
        pos = ((flat[0] + (k - 1)) * block + iota((block, 1), 0)).astype(F32)
        same = jnp.logical_and(low <= pos, pos < high)
        kern = jnp.where(same, kern, 0.0).astype(BF16)
        part = jnp.dot(data[V0:P0], kern, preferred_element_type=F32)
        total = part if total is None else total + part
    out[...] = own[2:3] * total + own[3:4] * mid[V0:P0].astype(F32)


def swap_norm(extra):
    e = extra.astype(F32)
    n = e.shape[1]
    sub = iota((16, n), 0)
    out = jnp.where(jnp.logical_and(sub > 2, sub < 6), 1.0, 0.0)
    for k in range(3):
        out = jnp.where(sub == k, e[k + 3 : k + 4], out)
    return out.astype(BF16)


def image_kernel(sa, sb, diag, mid, image, stats):
    parts = [jnp.sum(ref[...].astype(F32), axis=0) for ref in (sa, sb)]
    img = jnp.concatenate(parts, axis=1) + diag[...]
    image[...] = img
    v = mid[V0:P0].astype(F32)
    vv = jnp.sum(v * v, axis=1, keepdims=True)
    vi = jnp.sum(v * img, axis=1, keepdims=True)
    ratio = jnp.where(vv > 0.0, vi / jnp.where(vv > 0.0, vv, 1.0), 0.0)
    rest = img - ratio * v
    rr = jnp.sum(rest * rest, axis=1, keepdims=True)
    lane = iota((32, 128), 1)
    wide = jnp.where(lane == 0, vv, jnp.where(lane == 1, vi, jnp.where(lane == 2, rr, 0.0)))
    turned = wide.T
    row = jnp.concatenate(
        [turned[0:1], turned[1:2], turned[2:3], jnp.zeros((1, 32), F32)], axis=1
    )
    for d in range(stats.shape[0]):
        stats[d] = row


def final_kernel(stats, image, mid, residual, direction, alpha_out, beta_out):
    every = stats[...]
    every = every.reshape(every.shape[0], 128)
    vv, vi, rr = every[:, 0:32], every[:, 32:64], every[:, 64:96]
    total_v = jnp.sum(vv, axis=0, keepdims=True)
    total_i = jnp.sum(vi, axis=0, keepdims=True)
    center = total_i / total_v
    ratio = jnp.where(vv > 0.0, vi / jnp.where(vv > 0.0, vv, 1.0), 0.0)
    shift = ratio - center
    total_r = jnp.sum(rr + vv * (shift * shift), axis=0, keepdims=True)
    alpha = total_v / total_i
    beta = alpha * alpha * total_r / total_v
    alpha_out[...] = alpha
    beta_out[...] = beta
    v = mid[V0:P0].astype(F32).T
    res = v - alpha * image[...].T
    residual[...] = res
    direction[...] = res + beta * v


def body(
    features,
    task_id,
    task_count,
    task_rank,
    probes,
    net_w,
    net_b,
    inv_scale,
    task_mix,
    task_diag,
    task_noise,
):
    rows = features.shape[0]
    n_row, n_col = lax.axis_size("row"), lax.axis_size("col")
    devices = n_row * n_col
    axes = ("row", "col")
    width = probes.shape[1]
    flat = (lax.axis_index("row") * n_col + lax.axis_index("col")).astype(jnp.int32).reshape(1)
    counts = task_count.reshape(1, -1)
    ntask = counts.shape[1]
    table = jnp.concatenate(
        [task_mix.T, task_diag[None], task_noise[None], jnp.zeros((2, ntask), F32)], axis=0
    )
    packed, payload = pl.pallas_call(
        pack_kernel,
        in_specs=[VMEM] * 8,
        out_specs=[VMEM, VMEM],
        out_shape=[jax.ShapeDtypeStruct((rows, 128), BF16)] * 2,
        compiler_params=PARAMS,
        name="pack",
    )(
        features,
        task_id.reshape(1, -1),
        counts,
        task_rank.reshape(1, -1),
        probes,
        net_w,
        net_b.reshape(1, -1),
        inv_scale.reshape(1, -1),
    )
    got = lax.all_to_all(packed, axes, split_axis=0, concat_axis=0, tiled=True)
    chunks = [payload] + [
        lax.ppermute(payload, "row", [(i, (i + k) % n_row) for i in range(n_row)])
        for k in range(1, n_row)
    ]
    half = rows // 2
    rows_w, own = pl.pallas_call(
        functools.partial(rows_kernel, n_col),
        in_specs=[SMEM, VMEM, VMEM],
        out_specs=[VMEM, VMEM],
        out_shape=[
            jax.ShapeDtypeStruct((2, 8, n_col * half), F32),
            jax.ShapeDtypeStruct((8, rows), F32),
        ],
        compiler_params=PARAMS,
        cost_estimate=pl.CostEstimate(flops=1 << 30, bytes_accessed=1 << 20, transcendentals=0),
        name="rows",
    )(flat, counts, table)
    mid, za, zb = pl.pallas_call(
        sort_kernel,
        in_specs=[VMEM],
        out_specs=[VMEM] * 3,
        out_shape=[
            jax.ShapeDtypeStruct((P0, rows), BF16),
            jax.ShapeDtypeStruct((n_col, V0, half), BF16),
            jax.ShapeDtypeStruct((n_col, V0, half), BF16),
        ],
        compiler_params=PARAMS,
        name="sort",
    )(got)
    ga = lax.all_to_all(za, "col", split_axis=0, concat_axis=0, tiled=True)
    gb = lax.all_to_all(zb, "col", split_axis=0, concat_axis=0, tiled=True)
    prev = lax.ppermute(mid, axes, [(i, (i + 1) % devices) for i in range(devices)])
    nxt = lax.ppermute(mid, axes, [(i, (i - 1) % devices) for i in range(devices)])
    total = n_row * rows
    zc, st = pl.pallas_call(
        cols_kernel,
        in_specs=[VMEM] * (1 + n_row),
        out_specs=[VMEM, VMEM],
        out_shape=[
            jax.ShapeDtypeStruct((total, 128), BF16),
            jax.ShapeDtypeStruct((4 * width, total), BF16),
        ],
        compiler_params=PARAMS,
        cost_estimate=pl.CostEstimate(flops=1 << 31, bytes_accessed=4 << 20, transcendentals=0),
        name="cols",
    )(table, *chunks)
    pa = main_call(ga, rows_w[0], zc, st)
    sa = lax.all_to_all(pa, "col", split_axis=0, concat_axis=0, tiled=True)
    pb = main_call(gb, rows_w[1], zc, st)
    sb = lax.all_to_all(pb, "col", split_axis=0, concat_axis=0, tiled=True)
    diag = pl.pallas_call(
        same_kernel,
        in_specs=[SMEM, VMEM, VMEM, VMEM, VMEM],
        out_specs=VMEM,
        out_shape=jax.ShapeDtypeStruct((width, rows), F32),
        compiler_params=PARAMS,
        cost_estimate=pl.CostEstimate(flops=1 << 31, bytes_accessed=1 << 20, transcendentals=0),
        name="same",
    )(flat, own, mid, prev, nxt)
    image, stats = pl.pallas_call(
        image_kernel,
        in_specs=[VMEM] * 4,
        out_specs=[VMEM] * 2,
        out_shape=[
            jax.ShapeDtypeStruct((width, rows), F32),
            jax.ShapeDtypeStruct((devices, 1, 128), F32),
        ],
        compiler_params=PARAMS,
        name="image",
    )(sa, sb, diag, mid)
    every = lax.all_to_all(stats, axes, split_axis=0, concat_axis=0, tiled=True)
    residual, direction, alpha, beta = pl.pallas_call(
        final_kernel,
        in_specs=[VMEM] * 3,
        out_specs=[VMEM] * 4,
        out_shape=[
            jax.ShapeDtypeStruct((rows, width), F32),
            jax.ShapeDtypeStruct((rows, width), F32),
            jax.ShapeDtypeStruct((1, width), F32),
            jax.ShapeDtypeStruct((1, width), F32),
        ],
        compiler_params=PARAMS,
        name="final",
    )(every, image, mid)
    return residual, direction, alpha.reshape(width), beta.reshape(width)


def solution(mesh):
    axes = ("row", "col")
    return jax.shard_map(
        body,
        mesh=mesh,
        in_specs=(
            P(axes, None),
            P(axes),
            P(),
            P(axes),
            P(axes, None),
            P(),
            P(),
            P(),
            P(),
            P(),
            P(),
        ),
        out_specs=(P(axes, None), P(axes, None), P(), P()),
        check_vma=False,
    )
```

```python
import functools

import jax
import jax.numpy as jnp
from jax import lax
from jax.experimental import pallas as pl
from jax.experimental.pallas import tpu as pltpu
from jax.sharding import PartitionSpec as P

F32 = jnp.float32
BF16 = jnp.bfloat16
VMEM = pl.BlockSpec(memory_space=pltpu.VMEM)
SMEM = pl.BlockSpec(memory_space=pltpu.SMEM)
PARAMS = pltpu.CompilerParams(vmem_limit_bytes=16 * 1024 * 1024)
LARGE = pltpu.CompilerParams(vmem_limit_bytes=40 * 1024 * 1024)
V0, T0, P0, N0 = 64, 96, 97, 99
TASK = 70


def iota(shape, dim):
    return lax.broadcasted_iota(jnp.int32, shape, dim)


def split3(x):
    hi = x.astype(BF16)
    rest = x - hi.astype(F32)
    mid = rest.astype(BF16)
    low = (rest - mid.astype(F32)).astype(BF16)
    return hi, mid, low


def look_up(table, task):
    hit = (iota((table.shape[1], task.shape[1]), 0) == task).astype(BF16)
    tab = jnp.concatenate(split3(table), axis=0)
    got = jnp.dot(tab, hit, preferred_element_type=F32)
    return got[0:8] + got[8:16] + got[16:24]


def pack_kernel(
    feat, tid, cnt, rank, probes, net_w, net_b, scale, table, cols, rows_out, vq_out, nv_out, pos_out
):
    rows = feat.shape[1]
    ntask = cnt.shape[1]
    width = probes.shape[0]
    counts = cnt[...].astype(F32)
    before = iota((ntask, ntask), 1) < iota((ntask, ntask), 0)
    start = jnp.sum(jnp.where(before, counts, 0.0), axis=1, keepdims=True)
    task = tid[...]
    hit = iota((ntask, rows), 0) == task
    pos = jnp.sum(jnp.where(hit, start, 0.0), axis=0, keepdims=True) + rank[...].astype(F32)
    pos_col = jnp.concatenate([pos, jnp.zeros((7, rows), F32)], axis=0).T[:, 0:1]
    order = jnp.sum((pos_col < pos).astype(F32), axis=0, keepdims=True)
    tile = jnp.floor(order * (1.0 / 64.0))
    inner = order - tile * 64.0
    block = jnp.floor(inner * 0.25)
    order_r = tile * 64.0 + (inner - block * 4.0) * 16.0 + block
    square = iota((rows, rows), 0)
    place_c = (square == order.astype(jnp.int32)).astype(BF16)
    place_r = (square == order_r.astype(jnp.int32)).astype(BF16)
    column = jnp.concatenate([net_b[...], scale[...], jnp.zeros((6, 64), F32)], axis=0).T
    hidden = jnp.tanh(
        lax.dot_general(
            net_w[...], feat[...], (((0,), (0,)), ((), ())), preferred_element_type=F32
        )
        + column[:, 0:1]
    )
    latent = (hidden * column[:, 1:2]).astype(BF16)
    local = pos - jnp.floor(pos * (1.0 / rows)) * rows
    high = jnp.floor(local * (1.0 / 16.0))
    noise = look_up(table[...], task)[5:6]
    extra = jnp.concatenate(
        [task.astype(F32), high, local - 16.0 * high]
        + [a.astype(F32) for a in split3(noise)]
        + [jnp.zeros((26, rows), F32)],
        axis=0,
    ).astype(BF16)
    whole = jnp.concatenate([latent, probes[...], extra], axis=0)
    turn = (((1,), (1,)), ((), ()))
    cols[...] = lax.dot_general(place_c, whole, turn, preferred_element_type=F32).astype(BF16)
    data = lax.dot_general(place_r, whole, turn, preferred_element_type=F32)
    half = rows // 2
    pair = jnp.concatenate([data[:half, :V0], data[half:, :V0]], axis=1).astype(BF16)
    at = (iota((16, rows), 1) % 16 == iota((16, rows), 0)).astype(BF16)
    group = jnp.where(iota((rows, 128), 0) // 16 == iota((rows, 128), 1), data[:, T0 : T0 + 1], 0.0)
    tasks = jnp.dot(at, group.astype(BF16), preferred_element_type=F32).astype(BF16)
    for k in range(rows_out.shape[0]):
        rows_out[k, :half, :] = pair
        rows_out[k, half:, :] = tasks
    place = data[:, P0 : P0 + 1] * 16.0 + data[:, P0 + 1 : P0 + 2]
    noise_c = data[:, N0 : N0 + 1] + data[:, N0 + 1 : N0 + 2] + data[:, N0 + 2 : N0 + 3]
    v = data[:, V0:T0]
    nv = noise_c * v

    def fold(x, m):
        return jnp.concatenate(
            [x[t * 64 + m * 16 : t * 64 + m * 16 + 16] for t in range(rows // 64)], axis=0
        )

    vq_out[...] = jnp.concatenate([fold(v, m) for m in range(4)], axis=1)
    nv_out[...] = jnp.concatenate([fold(nv, m) for m in range(4)], axis=1)
    lane = iota((rows // 4, 128), 1)
    posq = jnp.zeros((rows // 4, 128), F32)
    for m in range(4):
        posq = jnp.where(lane == 3 * width + m, fold(place, m), posq)
    pos_out[...] = posq


def cols_kernel(table, *refs):
    chunks, (zc, st) = refs[:-2], refs[-2:]
    rows = chunks[0].shape[0]
    count = len(chunks)
    size = 4 * 16 * count
    width = T0 - V0
    for k in range(rows // 64):
        data = jnp.concatenate(
            [ref[g * 16 : g * 16 + 16, :] for g in range(4 * k, 4 * k + 4) for ref in chunks],
            axis=0,
        ).astype(F32)
        span = slice(k * size, (k + 1) * size)
        lane = iota((size, 128), 1)
        z = jnp.where(lane < V0, data, 0.0)
        norm = jnp.sum(z * z, axis=1, keepdims=True) * -0.5
        hi, mid, low = (a.astype(F32) for a in split3(norm))
        z = jnp.where(lane == V0, hi, z)
        z = jnp.where(lane == V0 + 1, mid, z)
        z = jnp.where(lane == V0 + 2, low, z)
        z = jnp.where(jnp.logical_and(lane > V0 + 2, lane < V0 + 6), 1.0, z)
        z = jnp.where(lane == TASK, data[:, T0 : T0 + 1], z)
        zc[span, :] = z.astype(BF16)
        turned = data.T
        weight = look_up(table[...], turned[T0 : T0 + 1].astype(jnp.int32))
        values = turned[V0:T0]
        for q in range(4):
            st[q * width : (q + 1) * width, span] = (weight[q : q + 1] * values).astype(BF16)
        st[4 * width :, span] = values.astype(BF16)


def product_kernel(tile, own_col, table, zr, ext, zc, st, out, own, kern_ref, task_ref, mine):
    t = pl.program_id(0)
    n_col = zr.shape[0]
    wide = n_col * 16
    rows = 4 * wide

    @pl.when(t == 0)
    def _():
        every = ext[...].reshape(wide, 128).astype(F32).T
        for k in range(task_ref.shape[0]):
            task_ref[k] = every[4 * k : 4 * k + 8]

    data = jnp.concatenate(
        [zr[k, m * 16 : m * 16 + 16, :] for m in range(4) for k in range(n_col)], axis=0
    )
    turned = data.astype(F32).T
    z = jnp.where(t < pl.num_programs(0) // 2, turned[:V0], turned[V0:])
    norm = jnp.sum(z * z, axis=0, keepdims=True) * -0.5
    hi, mid, low = (a.astype(F32) for a in split3(norm))
    sub = iota((16, rows), 0)
    extra = jnp.where(sub < 3, 1.0, 0.0)
    extra = jnp.where(sub == 3, hi, extra)
    extra = jnp.where(sub == 4, mid, extra)
    extra = jnp.where(sub == 5, low, extra)
    z = jnp.concatenate([z, extra, jnp.zeros((48, rows), F32)], axis=0).astype(BF16)
    four = task_ref[t]
    task = jnp.concatenate([four[m : m + 1] for m in range(4)], axis=1)
    weight = look_up(table[...], task.astype(jnp.int32))
    width = st.shape[0] // 5
    total = None
    for j in range(zc.shape[0] // tile):
        span = slice(j * tile, (j + 1) * tile)
        x = jnp.dot(zc[span, :], z, preferred_element_type=F32)
        kern = jnp.minimum(jnp.exp(x).astype(BF16), jnp.asarray(1.0, BF16))
        kern_ref[span, :] = kern
        part = jnp.dot(st[: 4 * width, span], kern, preferred_element_type=F32)
        total = part if total is None else total + part
    size = zc.shape[0] // 32
    first = pl.multiple_of(jnp.clip(4 * t - 1, 0, 26) * size, size)
    band = pl.ds(first, 6 * size)
    same = zc[band, TASK : TASK + 1] == task.astype(BF16)
    kept = jnp.where(same, kern_ref[band, :], jnp.asarray(0.0, BF16))
    summed = weight[4:5] * jnp.dot(st[4 * width :, band], kept, preferred_element_type=F32)
    for q in range(4):
        summed = summed + weight[q : q + 1] * total[q * width : (q + 1) * width]
    folded = jnp.concatenate(
        [summed[:, m * wide : (m + 1) * wide] for m in range(4)], axis=0
    ).T.reshape(n_col, 16, 128)
    out[...] = folded.astype(out.dtype)
    mine[...] = folded
    own[...] = mine[own_col[0]]


def product_call(col, table, gathered, zc, st):
    n_col, packed, _ = gathered.shape
    cols = zc.shape[0]
    width = st.shape[0] // 5
    tiles = (packed - 16) // 32
    rows = n_col * 64
    return pl.pallas_call(
        functools.partial(product_kernel, 1024),
        grid=(tiles,),
        in_specs=[
            SMEM,
            pl.BlockSpec(table.shape, lambda i: (0, 0)),
            pl.BlockSpec((n_col, 64, 128), lambda i: (0, i % (tiles // 2), 0)),
            pl.BlockSpec((n_col, 16, 128), lambda i: (0, tiles * 2, 0)),
            pl.BlockSpec((cols, 128), lambda i: (0, 0)),
            pl.BlockSpec((st.shape[0], cols), lambda i: (0, 0)),
        ],
        out_specs=[
            pl.BlockSpec((n_col, 16, 128), lambda i: (0, i, 0)),
            pl.BlockSpec((16, 128), lambda i: (i, 0)),
        ],
        out_shape=[
            jax.ShapeDtypeStruct((n_col, tiles * 16, 128), BF16),
            jax.ShapeDtypeStruct((tiles * 16, 128), F32),
        ],
        scratch_shapes=[
            pltpu.VMEM((cols, rows), BF16),
            pltpu.VMEM((tiles, 8, n_col * 16), F32),
            pltpu.VMEM((n_col, 16, 128), F32),
        ],
        compiler_params=LARGE,
        cost_estimate=pl.CostEstimate(
            flops=2 * tiles * rows * cols * 512, bytes_accessed=4 << 20, transcendentals=0
        ),
        name="product",
    )(col, table, gathered, gathered, zc, st)


def image_kernel(col, parts, own, vq, nv, pos, send):
    n_col = parts.shape[0]
    img = own[...] + nv[...]
    for k in range(n_col):
        img = img + jnp.where(k == col[0], 0.0, parts[k].astype(F32))
    v = vq[...]

    def over(x):
        s = jnp.sum(x, axis=0, keepdims=True)
        return s[:, 0:32] + s[:, 32:64] + s[:, 64:96] + s[:, 96:128]

    vv, vi = over(v * v), over(v * img)
    ratio = jnp.where(vv > 0.0, vi / jnp.where(vv > 0.0, vv, 1.0), 0.0)
    rest = img - jnp.concatenate([ratio] * 4, axis=1) * v
    row = jnp.concatenate([vv, vi, over(rest * rest), jnp.zeros_like(vv)], axis=1)
    send[:, 0, :] = img
    send[:, 1, :] = v
    send[:, 2, :] = pos[...] + row


def final_kernel(got, residual, direction, alpha_out, beta_out):
    n = got.shape[0]
    rows = residual.shape[1]
    img, v, every = got[:, 0, :], got[:, 1, :], got[:, 2, :]
    vv, vi, rr = every[:, 0:32], every[:, 32:64], every[:, 64:96]
    total_v = jnp.sum(vv, axis=0, keepdims=True)
    total_i = jnp.sum(vi, axis=0, keepdims=True)
    center = total_i / total_v
    ratio = jnp.where(vv > 0.0, vi / jnp.where(vv > 0.0, vv, 1.0), 0.0)
    shift = ratio - center
    total_r = jnp.sum(rr + vv * (shift * shift), axis=0, keepdims=True)
    alpha = total_v / total_i
    beta = alpha * alpha * total_r / total_v
    alpha_out[...] = alpha
    beta_out[...] = beta
    res = v - jnp.concatenate([alpha] * 4, axis=1) * img
    pieces = split3(res) + (v.astype(BF16),)
    total = None
    for m in range(4):
        lanes = slice(m * 32, (m + 1) * 32)
        values = jnp.concatenate([p[:, lanes] for p in pieces], axis=1)
        place = every[:, 96 + m : 97 + m].astype(jnp.int32)
        onehot = (iota((n, rows), 1) == place).astype(BF16)
        part = lax.dot_general(
            values, onehot, (((0,), (0,)), ((), ())), preferred_element_type=F32
        )
        total = part if total is None else total + part
    res_t = total[0:32] + total[32:64] + total[64:96]
    residual[...] = res_t
    beta_col = jnp.concatenate([beta, jnp.zeros((7, 32), F32)], axis=0).T[:, 0:1]
    direction[...] = res_t + beta_col * total[96:128]


def body(
    features,
    task_id,
    task_count,
    task_rank,
    probes,
    net_w,
    net_b,
    inv_scale,
    task_mix,
    task_diag,
    task_noise,
):
    rows, feat = features.shape
    n_row, n_col = lax.axis_size("row"), lax.axis_size("col")
    devices = n_row * n_col
    width = probes.shape[1]
    quarter = rows // 4
    col = lax.axis_index("col").astype(jnp.int32).reshape(1)
    ntask = task_count.shape[0]
    table = jnp.concatenate(
        [task_mix.T, task_diag[None], task_noise[None], jnp.zeros((2, ntask), F32)], axis=0
    )
    mine, share, vq, nv, pos = pl.pallas_call(
        pack_kernel,
        in_specs=[VMEM] * 9,
        out_specs=[VMEM] * 5,
        out_shape=[
            jax.ShapeDtypeStruct((rows, 128), BF16),
            jax.ShapeDtypeStruct((n_col, rows // 2 + 16, 128), BF16),
            jax.ShapeDtypeStruct((quarter, 128), F32),
            jax.ShapeDtypeStruct((quarter, 128), F32),
            jax.ShapeDtypeStruct((quarter, 128), F32),
        ],
        compiler_params=PARAMS,
        name="pack",
    )(
        features.T,
        task_id.reshape(1, -1),
        task_count.reshape(1, -1),
        task_rank.reshape(1, -1),
        probes.T,
        net_w,
        net_b.reshape(1, -1),
        inv_scale.reshape(1, -1),
        table,
    )
    chunks = [mine] + [
        lax.ppermute(mine, "row", [(i, (i + k) % n_row) for i in range(n_row)])
        for k in range(1, n_row)
    ]
    gathered = lax.all_to_all(share, "col", split_axis=0, concat_axis=0, tiled=True)
    total = n_row * rows
    zc, st = pl.pallas_call(
        cols_kernel,
        in_specs=[VMEM] * (1 + n_row),
        out_specs=[VMEM, VMEM],
        out_shape=[
            jax.ShapeDtypeStruct((total, 128), BF16),
            jax.ShapeDtypeStruct((5 * width, total), BF16),
        ],
        compiler_params=PARAMS,
        cost_estimate=pl.CostEstimate(flops=1 << 31, bytes_accessed=4 << 20, transcendentals=0),
        name="cols",
    )(table, *chunks)
    parts, own = product_call(col, table, gathered, zc, st)
    summed = lax.all_to_all(parts, "col", split_axis=0, concat_axis=0, tiled=True)
    send = pl.pallas_call(
        image_kernel,
        in_specs=[SMEM] + [VMEM] * 5,
        out_specs=VMEM,
        out_shape=jax.ShapeDtypeStruct((devices, 3, 128), F32),
        compiler_params=PARAMS,
        name="image",
    )(col, summed, own, vq, nv, pos)
    got = lax.all_to_all(send, ("row", "col"), split_axis=0, concat_axis=0, tiled=True)
    residual, direction, alpha, beta = pl.pallas_call(
        final_kernel,
        in_specs=[VMEM],
        out_specs=[VMEM] * 4,
        out_shape=[
            jax.ShapeDtypeStruct((width, rows), F32),
            jax.ShapeDtypeStruct((width, rows), F32),
            jax.ShapeDtypeStruct((1, width), F32),
            jax.ShapeDtypeStruct((1, width), F32),
        ],
        compiler_params=PARAMS,
        name="final",
    )(got)
    return residual.T, direction.T, alpha.reshape(width), beta.reshape(width)


def solution(mesh):
    axes = ("row", "col")
    return jax.shard_map(
        body,
        mesh=mesh,
        in_specs=(
            P(axes, None),
            P(axes),
            P(),
            P(axes),
            P(axes, None),
            P(),
            P(),
            P(),
            P(),
            P(),
            P(),
        ),
        out_specs=(P(axes, None), P(axes, None), P(), P()),
        check_vma=False,
    )
```

```python
import functools
import math

import jax
import jax.numpy as jnp
from jax import lax
from jax.experimental import pallas as pl
from jax.experimental.pallas import tpu as pltpu
from jax.sharding import PartitionSpec as P

F32 = jnp.float32
BF16 = jnp.bfloat16
VMEM = pl.BlockSpec(memory_space=pltpu.VMEM)
SMEM = pl.BlockSpec(memory_space=pltpu.SMEM)
PARAMS = pltpu.CompilerParams(vmem_limit_bytes=16 * 1024 * 1024)
ALONE = pltpu.CompilerParams(vmem_limit_bytes=60 * 1024 * 1024)
LARGE = pltpu.CompilerParams(vmem_limit_bytes=40 * 1024 * 1024)
V0, T0, P0, N0 = 64, 96, 97, 112
NORM, TASK = 192, 198
LOG2E = math.log2(math.e)


def iota(shape, dim):
    return lax.broadcasted_iota(jnp.int32, shape, dim)


def split3(x):
    hi = x.astype(BF16)
    rest = x - hi.astype(F32)
    mid = rest.astype(BF16)
    low = (rest - mid.astype(F32)).astype(BF16)
    return hi, mid, low


def look_up(table, task):
    hit = (iota((table.shape[1], task.shape[1]), 0) == task).astype(BF16)
    tab = jnp.concatenate(split3(table), axis=0)
    got = jnp.dot(tab, hit, preferred_element_type=F32)
    return got[0:8] + got[8:16] + got[16:24]


def order_of(tid, cnt, rank):
    rows, ntask = tid.shape[1], cnt.shape[1]
    counts = cnt[...].astype(F32)
    before = iota((ntask, ntask), 1) < iota((ntask, ntask), 0)
    start = jnp.sum(jnp.where(before, counts, 0.0), axis=1, keepdims=True)
    hit = iota((ntask, rows), 0) == tid[...]
    pos = jnp.sum(jnp.where(hit, start, 0.0), axis=0, keepdims=True) + rank[...].astype(F32)
    pos_col = jnp.concatenate([pos, jnp.zeros((7, rows), F32)], axis=0).T[:, 0:1]
    return pos, jnp.sum((pos_col < pos).astype(F32), axis=0, keepdims=True)


def pack_cols_kernel(feat, tid, cnt, rank, probes, net_w, net_b, scale, cols, whole_out, order_out):
    rows = feat.shape[1]
    pos, order = order_of(tid, cnt, rank)
    place = (iota((rows, rows), 0) == order.astype(jnp.int32)).astype(BF16)
    column = jnp.concatenate([net_b[...], scale[...], jnp.zeros((6, 64), F32)], axis=0).T
    hidden = jnp.tanh(
        lax.dot_general(
            net_w[...], feat[...], (((0,), (0,)), ((), ())), preferred_element_type=F32
        )
        + column[:, 0:1]
    )
    latent = (hidden * column[:, 1:2]).astype(BF16)
    local = pos - jnp.floor(pos * (1.0 / rows)) * rows
    high = jnp.floor(local * (1.0 / 16.0))
    extra = jnp.concatenate(
        [tid[...].astype(F32), high, local - 16.0 * high, jnp.zeros((29, rows), F32)], axis=0
    ).astype(BF16)
    whole = jnp.concatenate([latent, probes[...], extra], axis=0)
    whole_out[...] = whole
    order_out[...] = jnp.concatenate([order, jnp.zeros((7, rows), F32)], axis=0)
    cols[...] = lax.dot_general(
        place, whole, (((1,), (1,)), ((), ())), preferred_element_type=F32
    ).astype(BF16)


def pack_rows_kernel(whole, order_in, table, rows_out, vq_out, nv_out, pos_out):
    rows = whole.shape[1]
    width = T0 - V0
    order = order_in[0:1]
    tile = jnp.floor(order * (1.0 / 64.0))
    inner = order - tile * 64.0
    block = jnp.floor(inner * 0.25)
    order_r = tile * 64.0 + (inner - block * 4.0) * 16.0 + block
    place_r = (iota((rows, rows), 0) == order_r.astype(jnp.int32)).astype(BF16)
    noise = look_up(table[...], whole[T0 : T0 + 1].astype(jnp.int32))[5:6]
    noise = jnp.concatenate(split3(noise) + (jnp.zeros((13, rows), BF16),), axis=0)
    data = lax.dot_general(
        place_r,
        jnp.concatenate([whole[: T0 + 16], noise], axis=0),
        (((1,), (1,)), ((), ())),
        preferred_element_type=F32,
    )
    half = rows // 2
    pair = jnp.concatenate([data[:half, :V0], data[half:, :V0]], axis=1).astype(BF16)
    at = (iota((16, rows), 1) % 16 == iota((16, rows), 0)).astype(BF16)
    group = jnp.where(iota((rows, 128), 0) // 16 == iota((rows, 128), 1), data[:, T0 : T0 + 1], 0.0)
    tasks = jnp.dot(at, group.astype(BF16), preferred_element_type=F32).astype(BF16)
    for k in range(rows_out.shape[0]):
        rows_out[k, :half, :] = pair
        rows_out[k, half:, :] = tasks
    place = data[:, P0 : P0 + 1] * 16.0 + data[:, P0 + 1 : P0 + 2]
    noise_c = data[:, N0 : N0 + 1] + data[:, N0 + 1 : N0 + 2] + data[:, N0 + 2 : N0 + 3]
    v = data[:, V0:T0]
    nv = noise_c * v

    def fold(x, m):
        return jnp.concatenate(
            [x[t * 64 + m * 16 : t * 64 + m * 16 + 16] for t in range(rows // 64)], axis=0
        )

    vq_out[...] = jnp.concatenate([fold(v, m) for m in range(4)], axis=1)
    nv_out[...] = jnp.concatenate([fold(nv, m) for m in range(4)], axis=1)
    lane = iota((rows // 4, 128), 1)
    posq = jnp.zeros((rows // 4, 128), F32)
    for m in range(4):
        posq = jnp.where(lane == 3 * width + m, fold(place, m), posq)
    pos_out[...] = posq


def cols_kernel(table, *refs):
    chunks, (zc, st) = refs[:-2], refs[-2:]
    rows = chunks[0].shape[0]
    count = len(chunks)
    size = 4 * 16 * count
    width = T0 - V0
    for k in range(rows // 64):
        data = jnp.concatenate(
            [ref[g * 16 : g * 16 + 16, :] for g in range(4 * k, 4 * k + 4) for ref in chunks],
            axis=0,
        ).astype(F32)
        span = slice(k * size, (k + 1) * size)
        lane = iota((size, 128), 1)
        z = jnp.where(lane < V0, data, 0.0)
        norm = jnp.sum(z * z, axis=1, keepdims=True) * (-0.5 * LOG2E)
        hi, mid, low = (p.astype(F32) for p in split3(z * LOG2E))
        zc[span, :128] = (hi + pltpu.roll(mid, V0, 1)).astype(BF16)
        hi, mid, task = (p.astype(F32) for p in split3(norm))
        low = jnp.where(lane == NORM - 128, hi, low)
        low = jnp.where(lane == NORM - 127, mid, low)
        low = jnp.where(lane == NORM - 126, task, low)
        low = jnp.where(jnp.logical_and(lane > NORM - 126, lane < NORM - 122), 1.0, low)
        zc[span, 128:] = jnp.where(lane == TASK - 128, data[:, T0 : T0 + 1], low).astype(BF16)
        turned = data.T
        weight = look_up(table[...], turned[T0 : T0 + 1].astype(jnp.int32))
        values = turned[V0:T0]
        for q in range(4):
            st[q * width : (q + 1) * width, span] = (weight[q : q + 1] * values).astype(BF16)
        st[4 * width :, span] = values.astype(BF16)


def product_kernel(tile, own_col, table, zr, ext, zc, st, out, own, kern_ref, task_ref, mine):
    t = pl.program_id(0)
    n_col = zr.shape[0]
    wide = n_col * 16
    rows = 4 * wide

    @pl.when(t == 0)
    def _():
        every = ext[...].reshape(wide, 128).astype(F32).T
        for k in range(task_ref.shape[0]):
            task_ref[k] = every[4 * k : 4 * k + 8]

    data = jnp.concatenate(
        [zr[k, m * 16 : m * 16 + 16, :] for m in range(4) for k in range(n_col)], axis=0
    )
    turned = data.astype(F32).T
    z = jnp.where(t < pl.num_programs(0) // 2, turned[:V0], turned[V0:])
    norm = jnp.sum(z * z, axis=0, keepdims=True) * (-0.5 * LOG2E)
    hi, mid, low = (a.astype(F32) for a in split3(norm))
    sub = iota((16, rows), 0)
    extra = jnp.where(sub < 3, 1.0, 0.0)
    extra = jnp.where(sub == 3, hi, extra)
    extra = jnp.where(sub == 4, mid, extra)
    extra = jnp.where(sub == 5, low, extra)
    z = z.astype(BF16)
    z = jnp.concatenate([z, z, z, extra.astype(BF16), jnp.zeros((48, rows), BF16)], axis=0)
    four = task_ref[t]
    task = jnp.concatenate([four[m : m + 1] for m in range(4)], axis=1)
    weight = look_up(table[...], task.astype(jnp.int32))
    width = st.shape[0] // 5
    total = None
    for j in range(zc.shape[0] // tile):
        span = slice(j * tile, (j + 1) * tile)
        x = jnp.dot(zc[span, :], z, preferred_element_type=F32)
        kern = jnp.minimum(jnp.exp2(x).astype(BF16), jnp.asarray(1.0, BF16))
        kern_ref[span, :] = kern
        part = jnp.dot(st[: 4 * width, span], kern, preferred_element_type=F32)
        total = part if total is None else total + part
    size = zc.shape[0] // 32
    first = pl.multiple_of(jnp.clip(4 * t - 1, 0, 26) * size, size)
    band = pl.ds(first, 6 * size)
    same = zc[band, TASK : TASK + 1] == task.astype(BF16)
    kept = jnp.where(same, kern_ref[band, :], jnp.asarray(0.0, BF16))
    summed = weight[4:5] * jnp.dot(st[4 * width :, band], kept, preferred_element_type=F32)
    for q in range(4):
        summed = summed + weight[q : q + 1] * total[q * width : (q + 1) * width]
    folded = jnp.concatenate(
        [summed[:, m * wide : (m + 1) * wide] for m in range(4)], axis=0
    ).T.reshape(n_col, 16, 128)
    out[...] = folded.astype(out.dtype)
    mine[...] = folded
    own[...] = mine[own_col[0]]


def product_call(col, table, gathered, zc, st):
    n_col, packed, _ = gathered.shape
    cols = zc.shape[0]
    width = st.shape[0] // 5
    tiles = (packed - 16) // 32
    rows = n_col * 64
    return pl.pallas_call(
        functools.partial(product_kernel, 1024),
        grid=(tiles,),
        in_specs=[
            SMEM,
            pl.BlockSpec(table.shape, lambda i: (0, 0)),
            pl.BlockSpec((n_col, 64, 128), lambda i: (0, i % (tiles // 2), 0)),
            pl.BlockSpec((n_col, 16, 128), lambda i: (0, tiles * 2, 0)),
            pl.BlockSpec(zc.shape, lambda i: (0, 0)),
            pl.BlockSpec((st.shape[0], cols), lambda i: (0, 0)),
        ],
        out_specs=[
            pl.BlockSpec((n_col, 16, 128), lambda i: (0, i, 0)),
            pl.BlockSpec((16, 128), lambda i: (i, 0)),
        ],
        out_shape=[
            jax.ShapeDtypeStruct((n_col, tiles * 16, 128), BF16),
            jax.ShapeDtypeStruct((tiles * 16, 128), F32),
        ],
        scratch_shapes=[
            pltpu.VMEM((cols, rows), BF16),
            pltpu.VMEM((tiles, 8, n_col * 16), F32),
            pltpu.VMEM((n_col, 16, 128), F32),
        ],
        compiler_params=LARGE,
        cost_estimate=pl.CostEstimate(
            flops=2 * tiles * rows * cols * 512, bytes_accessed=4 << 20, transcendentals=0
        ),
        name="product",
    )(col, table, gathered, gathered, zc, st)


def image_kernel(col, parts, own, vq, nv, pos, send):
    n_col = parts.shape[0]
    img = own[...] + nv[...]
    for k in range(n_col):
        img = img + jnp.where(k == col[0], 0.0, parts[k].astype(F32))
    v = vq[...]

    def over(x):
        s = jnp.sum(x, axis=0, keepdims=True)
        return s[:, 0:32] + s[:, 32:64] + s[:, 64:96] + s[:, 96:128]

    vv, vi = over(v * v), over(v * img)
    ratio = jnp.where(vv > 0.0, vi / jnp.where(vv > 0.0, vv, 1.0), 0.0)
    rest = img - jnp.concatenate([ratio] * 4, axis=1) * v
    row = jnp.concatenate([vv, vi, over(rest * rest), jnp.zeros_like(vv)], axis=1)
    send[:, 0, :] = img
    send[:, 1, :] = v
    send[:, 2, :] = pos[...] + row


def final_kernel(got, residual, direction, alpha_out, beta_out):
    n = got.shape[0]
    rows = residual.shape[1]
    img, v, every = got[:, 0, :], got[:, 1, :], got[:, 2, :]
    vv, vi, rr = every[:, 0:32], every[:, 32:64], every[:, 64:96]
    total_v = jnp.sum(vv, axis=0, keepdims=True)
    total_i = jnp.sum(vi, axis=0, keepdims=True)
    center = total_i / total_v
    ratio = jnp.where(vv > 0.0, vi / jnp.where(vv > 0.0, vv, 1.0), 0.0)
    shift = ratio - center
    total_r = jnp.sum(rr + vv * (shift * shift), axis=0, keepdims=True)
    alpha = total_v / total_i
    beta = alpha * alpha * total_r / total_v
    alpha_out[...] = alpha
    beta_out[...] = beta
    res = v - jnp.concatenate([alpha] * 4, axis=1) * img
    pieces = split3(res) + (v.astype(BF16),)
    total = None
    for m in range(4):
        lanes = slice(m * 32, (m + 1) * 32)
        values = jnp.concatenate([p[:, lanes] for p in pieces], axis=1)
        place = every[:, 96 + m : 97 + m].astype(jnp.int32)
        onehot = (iota((n, rows), 1) == place).astype(BF16)
        part = lax.dot_general(
            values, onehot, (((0,), (0,)), ((), ())), preferred_element_type=F32
        )
        total = part if total is None else total + part
    res_t = total[0:32] + total[32:64] + total[64:96]
    residual[...] = res_t
    beta_col = jnp.concatenate([beta, jnp.zeros((7, 32), F32)], axis=0).T[:, 0:1]
    direction[...] = res_t + beta_col * total[96:128]


def body(
    features,
    task_id,
    task_count,
    task_rank,
    probes,
    net_w,
    net_b,
    inv_scale,
    task_mix,
    task_diag,
    task_noise,
):
    rows, feat = features.shape
    n_row, n_col = lax.axis_size("row"), lax.axis_size("col")
    devices = n_row * n_col
    width = probes.shape[1]
    quarter = rows // 4
    col = lax.axis_index("col").astype(jnp.int32).reshape(1)
    ntask = task_count.shape[0]
    table = jnp.concatenate(
        [task_mix.T, task_diag[None], task_noise[None], jnp.zeros((2, ntask), F32)], axis=0
    )
    mine, whole, order = pl.pallas_call(
        pack_cols_kernel,
        in_specs=[VMEM] * 8,
        out_specs=[VMEM] * 3,
        out_shape=[
            jax.ShapeDtypeStruct((rows, 128), BF16),
            jax.ShapeDtypeStruct((128, rows), BF16),
            jax.ShapeDtypeStruct((8, rows), F32),
        ],
        compiler_params=ALONE,
        name="pack_cols",
    )(
        features.T,
        task_id.reshape(1, -1),
        task_count.reshape(1, -1),
        task_rank.reshape(1, -1),
        probes.T,
        net_w,
        net_b.reshape(1, -1),
        inv_scale.reshape(1, -1),
    )
    chunks = [mine] + [
        lax.ppermute(mine, "row", [(i, (i + 2 * k) % n_row) for i in range(n_row)])
        for k in range(1, n_row // 2)
    ]
    chunks = chunks + [lax.ppermute(c, "row", [(i, i ^ 1) for i in range(n_row)]) for c in chunks]
    share, vq, nv, pos = pl.pallas_call(
        pack_rows_kernel,
        in_specs=[VMEM] * 3,
        out_specs=[VMEM] * 4,
        out_shape=[
            jax.ShapeDtypeStruct((n_col, rows // 2 + 16, 128), BF16),
            jax.ShapeDtypeStruct((quarter, 128), F32),
            jax.ShapeDtypeStruct((quarter, 128), F32),
            jax.ShapeDtypeStruct((quarter, 128), F32),
        ],
        compiler_params=PARAMS,
        name="pack_rows",
    )(whole, order, table)
    gathered = lax.all_to_all(share, "col", split_axis=0, concat_axis=0, tiled=True)
    total = n_row * rows
    zc, st = pl.pallas_call(
        cols_kernel,
        in_specs=[VMEM] * (1 + n_row),
        out_specs=[VMEM, VMEM],
        out_shape=[
            jax.ShapeDtypeStruct((total, 256), BF16),
            jax.ShapeDtypeStruct((5 * width, total), BF16),
        ],
        compiler_params=PARAMS,
        cost_estimate=pl.CostEstimate(flops=1 << 31, bytes_accessed=4 << 20, transcendentals=0),
        name="cols",
    )(table, *chunks)
    parts, own = product_call(col, table, gathered, zc, st)
    summed = lax.all_to_all(parts, "col", split_axis=0, concat_axis=0, tiled=True)
    send = pl.pallas_call(
        image_kernel,
        in_specs=[SMEM] + [VMEM] * 5,
        out_specs=VMEM,
        out_shape=jax.ShapeDtypeStruct((devices, 3, 128), F32),
        compiler_params=PARAMS,
        name="image",
    )(col, summed, own, vq, nv, pos)
    got = lax.all_to_all(send, ("row", "col"), split_axis=0, concat_axis=0, tiled=True)
    residual, direction, alpha, beta = pl.pallas_call(
        final_kernel,
        in_specs=[VMEM],
        out_specs=[VMEM] * 4,
        out_shape=[
            jax.ShapeDtypeStruct((width, rows), F32),
            jax.ShapeDtypeStruct((width, rows), F32),
            jax.ShapeDtypeStruct((1, width), F32),
            jax.ShapeDtypeStruct((1, width), F32),
        ],
        compiler_params=PARAMS,
        name="final",
    )(got)
    return residual.T, direction.T, alpha.reshape(width), beta.reshape(width)


def solution(mesh):
    axes = ("row", "col")
    return jax.shard_map(
        body,
        mesh=mesh,
        in_specs=(
            P(axes, None),
            P(axes),
            P(),
            P(axes),
            P(axes, None),
            P(),
            P(),
            P(),
            P(),
            P(),
            P(),
        ),
        out_specs=(P(axes, None), P(axes, None), P(), P()),
        check_vma=False,
    )
```

```python
import functools
import math

import jax
import jax.numpy as jnp
from jax import lax
from jax.experimental import pallas as pl
from jax.experimental.pallas import tpu as pltpu
from jax.sharding import PartitionSpec as P

F32 = jnp.float32
BF16 = jnp.bfloat16
VMEM = pl.BlockSpec(memory_space=pltpu.VMEM)
SMEM = pl.BlockSpec(memory_space=pltpu.SMEM)
PARAMS = pltpu.CompilerParams(vmem_limit_bytes=16 * 1024 * 1024)
ALONE = pltpu.CompilerParams(vmem_limit_bytes=60 * 1024 * 1024)
LARGE = pltpu.CompilerParams(vmem_limit_bytes=44 * 1024 * 1024)
V0, T0, N0, ONE, P0, S0 = 64, 96, 97, 100, 103, 112
LOG2E = math.log2(math.e)


def iota(shape, dim):
    return lax.broadcasted_iota(jnp.int32, shape, dim)


def split3(x):
    hi = x.astype(BF16)
    rest = x - hi.astype(F32)
    mid = rest.astype(BF16)
    low = (rest - mid.astype(F32)).astype(BF16)
    return hi, mid, low


def look_up(table, task):
    hit = (iota((table.shape[1], task.shape[1]), 0) == task).astype(BF16)
    tab = jnp.concatenate(split3(table), axis=0)
    got = jnp.dot(tab, hit, preferred_element_type=F32)
    return got[0:8] + got[8:16] + got[16:24]


def order_of(tid, cnt, rank):
    rows, ntask = tid.shape[1], cnt.shape[1]
    counts = cnt[...].astype(F32)
    before = iota((ntask, ntask), 1) < iota((ntask, ntask), 0)
    start = jnp.sum(jnp.where(before, counts, 0.0), axis=1, keepdims=True)
    hit = iota((ntask, rows), 0) == tid[...]
    pos = jnp.sum(jnp.where(hit, start, 0.0), axis=0, keepdims=True) + rank[...].astype(F32)
    pos_col = jnp.concatenate([pos, jnp.zeros((7, rows), F32)], axis=0).T[:, 0:1]
    return pos, jnp.sum((pos_col < pos).astype(F32), axis=0, keepdims=True)


def pack_kernel(
    feat, tid, cnt, rank, probes, net_w, net_b, scale, mix, diag, noise_in,
    cols, rows_out, vq_out, nv_out, pos_out, table_out,
):
    rows = feat.shape[1]
    width = probes.shape[0]
    pos, order = order_of(tid, cnt, rank)
    task = tid[...]
    table = jnp.concatenate(
        [mix[...], diag[...], noise_in[...], jnp.zeros((2, mix.shape[1]), F32)], axis=0
    )
    table_out[...] = table
    column = jnp.concatenate([net_b[...], scale[...], jnp.zeros((6, 64), F32)], axis=0).T
    hidden = jnp.tanh(
        lax.dot_general(
            net_w[...], feat[...], (((0,), (0,)), ((), ())), preferred_element_type=F32
        )
        + column[:, 0:1]
    )
    latent = (hidden * column[:, 1:2]).astype(BF16)
    lat = latent.astype(F32)
    norm = jnp.sum(lat * lat, axis=0, keepdims=True) * (-0.5 * LOG2E)
    local = pos - jnp.floor(pos * (1.0 / rows)) * rows
    high = jnp.floor(local * (1.0 / 16.0))
    noise = look_up(table, task)[5:6]
    extra = jnp.concatenate(
        [task.astype(F32)]
        + [a.astype(F32) for a in split3(norm)]
        + [jnp.ones((3, rows), F32), high, local - 16.0 * high, jnp.zeros((7, rows), F32)]
        + [a.astype(F32) for a in split3(noise)]
        + [jnp.zeros((13, rows), F32)],
        axis=0,
    ).astype(BF16)
    whole = jnp.concatenate([latent, probes[...], extra], axis=0)
    tile = jnp.floor(order * (1.0 / 64.0))
    inner = order - tile * 64.0
    block = jnp.floor(inner * 0.25)
    order_r = tile * 64.0 + (inner - block * 4.0) * 16.0 + block
    square = iota((rows, rows), 0)
    place_c = (square == order.astype(jnp.int32)).astype(BF16)
    place_r = (square == order_r.astype(jnp.int32)).astype(BF16)
    turn = (((1,), (1,)), ((), ()))
    data = lax.dot_general(place_c, whole, turn, preferred_element_type=F32).astype(BF16)
    for k in range(cols.shape[0]):
        cols[k] = data
    data = lax.dot_general(place_r, whole, turn, preferred_element_type=F32)
    half = rows // 2
    rows_out[:half, :] = jnp.concatenate([data[:half, :V0], data[half:, :V0]], axis=1).astype(BF16)
    at = (iota((16, rows), 1) % 16 == iota((16, rows), 0)).astype(BF16)
    group = jnp.where(iota((rows, 128), 0) // 16 == iota((rows, 128), 1), data[:, T0 : T0 + 1], 0.0)
    rows_out[half:, :] = jnp.dot(
        at, group.astype(BF16), preferred_element_type=F32
    ).astype(BF16)
    place = data[:, P0 : P0 + 1] * 16.0 + data[:, P0 + 1 : P0 + 2]
    noise_c = data[:, S0 : S0 + 1] + data[:, S0 + 1 : S0 + 2] + data[:, S0 + 2 : S0 + 3]
    v = data[:, V0:T0]
    nv = noise_c * v

    def fold(x, m):
        return jnp.concatenate(
            [x[t * 64 + m * 16 : t * 64 + m * 16 + 16] for t in range(rows // 64)], axis=0
        )

    vq_out[...] = jnp.concatenate([fold(v, m) for m in range(4)], axis=1)
    nv_out[...] = jnp.concatenate([fold(nv, m) for m in range(4)], axis=1)
    lane = iota((rows // 4, 128), 1)
    posq = jnp.zeros((rows // 4, 128), F32)
    for m in range(4):
        posq = jnp.where(lane == 3 * width + m, fold(place, m), posq)
    pos_out[...] = posq


def prepare_cols(table, cols, zc, st):
    chunks, rows, _ = cols.shape
    size = 4 * 16 * chunks
    width = T0 - V0
    for k in range(rows // 64):
        data = jnp.concatenate(
            [cols[h, g * 16 : g * 16 + 16, :] for g in range(4 * k, 4 * k + 4) for h in range(chunks)],
            axis=0,
        )
        span = slice(k * size, (k + 1) * size)
        wide = data.astype(F32)
        zc[span, 128:] = data
        zc[span, :128] = jnp.where(iota((size, 128), 1) < V0, wide, pltpu.roll(wide, V0, 1)).astype(BF16)
        turned = wide.T
        weight = look_up(table, turned[T0 : T0 + 1].astype(jnp.int32))
        values = turned[V0:T0]
        for q in range(4):
            st[q * width : (q + 1) * width, span] = (weight[q : q + 1] * values).astype(BF16)
        st[4 * width :, span] = values.astype(BF16)


def product_kernel(tile, chunks, table, cols, *refs):
    row_refs = refs[:chunks]
    near, far, kern_ref, task_ref, zc, st = refs[chunks:]
    i = pl.program_id(0)
    steps = pl.num_programs(0)
    tab = table[...]
    half = row_refs[0].shape[0] - 16

    @pl.when(i == 0)
    def _():
        every = jnp.concatenate([r[half:, :] for r in row_refs], axis=0).astype(F32).T
        for k in range(task_ref.shape[0]):
            task_ref[k] = every[8 * k : 8 * k + 8]
        prepare_cols(tab, cols, zc, st)

    first = pl.multiple_of(lax.rem(i, steps // 2) * 128, 128)
    blocks = [r[pl.ds(first, 128), :] for r in row_refs]
    data = jnp.concatenate(
        [b[g * 16 : g * 16 + 16, :] for g in range(8) for b in blocks], axis=0
    )
    rows = data.shape[0]
    turned = data.astype(F32).T
    z = jnp.where(i < steps // 2, turned[:V0], turned[V0:])
    norm = jnp.sum(z * z, axis=0, keepdims=True) * (-0.5 * LOG2E)
    parts = [a.astype(F32) for a in split3(norm)]
    sub = iota((T0 - V0, rows), 0)
    extra = jnp.where(jnp.logical_and(sub >= N0 - T0, sub < ONE - T0), 1.0, 0.0)
    for k in range(3):
        extra = jnp.where(sub == ONE - T0 + k, parts[k], extra)
    z = jnp.concatenate(
        split3(z * LOG2E) + (jnp.zeros((T0 - V0, rows), BF16), extra.astype(BF16)), axis=0
    )
    eight = task_ref[i]
    task = jnp.concatenate([eight[m : m + 1] for m in range(8)], axis=1)
    weight = look_up(tab, task.astype(jnp.int32))
    width = st.shape[0] // 5
    total = None
    for j in range(zc.shape[0] // tile):
        span = slice(j * tile, (j + 1) * tile)
        x = jnp.dot(zc[span, :], z, preferred_element_type=F32)
        kern = jnp.minimum(jnp.exp2(x).astype(BF16), jnp.asarray(1.0, BF16))
        kern_ref[span, :] = kern
        part = jnp.dot(st[: 4 * width, span], kern, preferred_element_type=F32)
        total = part if total is None else total + part
    low = weight[0:1] * total[:width]
    for q in range(1, 4):
        low = low + weight[q : q + 1] * total[q * width : (q + 1) * width]
    size = zc.shape[0] // 32
    count = rows // 2
    for k in range(2):
        lanes = slice(k * count, (k + 1) * count)
        start = pl.multiple_of(jnp.clip(4 * (2 * i + k) - 1, 0, 26) * size, size)
        band = pl.ds(start, 6 * size)
        same = zc[band, 128 + T0 : 129 + T0] == task[:, lanes].astype(BF16)
        kept = jnp.where(same, kern_ref[band, lanes], jnp.asarray(0.0, BF16))
        diag = jnp.dot(st[4 * width :, band], kept, preferred_element_type=F32)
        summed = low[:, lanes] + weight[4:5, lanes] * diag
        quarter = count // 4
        folded = jnp.concatenate(
            [summed[:, m * quarter : (m + 1) * quarter] for m in range(4)], axis=0
        ).T.reshape(chunks, 16, 128)
        near[:, k * 16 : k * 16 + 16, :] = folded[: chunks // 2]
        far[:, k * 16 : k * 16 + 16, :] = folded[chunks // 2 :]


def product_call(table, cols, row_parts):
    chunks = len(row_parts)
    total = cols.shape[0] * cols.shape[1]
    rows = cols.shape[1]
    steps = 4
    tile_rows = chunks * 128
    out = pl.BlockSpec((chunks // 2, 32, 128), lambda i: (0, i, 0))
    return pl.pallas_call(
        functools.partial(product_kernel, 2048, chunks),
        grid=(steps,),
        in_specs=[VMEM] * (2 + chunks),
        out_specs=[out, out],
        out_shape=[jax.ShapeDtypeStruct((chunks // 2, rows // 4, 128), F32)] * 2,
        scratch_shapes=[
            pltpu.VMEM((total, tile_rows), BF16),
            pltpu.VMEM((steps, 8, chunks * 16), F32),
            pltpu.VMEM((total, 256), BF16),
            pltpu.VMEM((5 * (T0 - V0), total), BF16),
        ],
        compiler_params=LARGE,
        cost_estimate=pl.CostEstimate(
            flops=2 * steps * tile_rows * total * 512, bytes_accessed=4 << 20, transcendentals=0
        ),
        name="product",
    )(table, cols, *row_parts)


def add_kernel(near, got, *out):
    for k, ref in enumerate(out):
        ref[...] = near[k] + got[k]


def image_kernel(nv, vq, pos, *refs):
    parts, send = refs[:-1], refs[-1]
    img = nv[...]
    for ref in parts:
        img = img + ref[...]
    v = vq[...]

    def over(x):
        s = jnp.sum(x, axis=0, keepdims=True)
        return s[:, 0:32] + s[:, 32:64] + s[:, 64:96] + s[:, 96:128]

    vv, vi = over(v * v), over(v * img)
    ratio = jnp.where(vv > 0.0, vi / jnp.where(vv > 0.0, vv, 1.0), 0.0)
    rest = img - jnp.concatenate([ratio] * 4, axis=1) * v
    row = jnp.concatenate([vv, vi, over(rest * rest), jnp.zeros_like(vv)], axis=1)
    send[:, 0, :] = img
    send[:, 1, :] = v
    send[:, 2, :] = pos[...] + row


def final_kernel(got, residual, direction, alpha_out, beta_out):
    n = got.shape[0]
    rows = residual.shape[1]
    img, v, every = got[:, 0, :], got[:, 1, :], got[:, 2, :]
    vv, vi, rr = every[:, 0:32], every[:, 32:64], every[:, 64:96]
    total_v = jnp.sum(vv, axis=0, keepdims=True)
    total_i = jnp.sum(vi, axis=0, keepdims=True)
    center = total_i / total_v
    ratio = jnp.where(vv > 0.0, vi / jnp.where(vv > 0.0, vv, 1.0), 0.0)
    shift = ratio - center
    total_r = jnp.sum(rr + vv * (shift * shift), axis=0, keepdims=True)
    alpha = total_v / total_i
    beta = alpha * alpha * total_r / total_v
    alpha_out[...] = alpha
    beta_out[...] = beta
    res = v - jnp.concatenate([alpha] * 4, axis=1) * img
    pieces = split3(res) + (v.astype(BF16),)
    total = None
    for m in range(4):
        lanes = slice(m * 32, (m + 1) * 32)
        values = jnp.concatenate([p[:, lanes] for p in pieces], axis=1)
        place = every[:, 96 + m : 97 + m].astype(jnp.int32)
        onehot = (iota((n, rows), 1) == place).astype(BF16)
        part = lax.dot_general(
            values, onehot, (((0,), (0,)), ((), ())), preferred_element_type=F32
        )
        total = part if total is None else total + part
    res_t = total[0:32] + total[32:64] + total[64:96]
    residual[...] = res_t
    beta_col = jnp.concatenate([beta, jnp.zeros((7, 32), F32)], axis=0).T[:, 0:1]
    direction[...] = res_t + beta_col * total[96:128]


def body(
    features,
    task_id,
    task_count,
    task_rank,
    probes,
    net_w,
    net_b,
    inv_scale,
    task_mix,
    task_diag,
    task_noise,
):
    rows = features.shape[0]
    n_row, n_col = lax.axis_size("row"), lax.axis_size("col")
    devices = n_row * n_col
    axes = ("row", "col")
    width = probes.shape[1]
    quarter = rows // 4
    n_y, n_x, n_z = n_row // 2, n_col // 4, 4
    shape = jax.ShapeDtypeStruct((quarter, 128), F32)
    cols, share, vq, nv, pos, table = pl.pallas_call(
        pack_kernel,
        in_specs=[VMEM] * 11,
        out_specs=[VMEM] * 6,
        out_shape=[
            jax.ShapeDtypeStruct((n_y * n_z, rows, 128), BF16),
            jax.ShapeDtypeStruct((rows // 2 + 16, 128), BF16),
            shape,
            shape,
            shape,
            jax.ShapeDtypeStruct((8, task_count.shape[0]), F32),
        ],
        compiler_params=ALONE,
        name="pack",
    )(
        features.T,
        task_id.reshape(1, -1),
        task_count.reshape(1, -1),
        task_rank.reshape(1, -1),
        probes.T,
        net_w,
        net_b.reshape(1, -1),
        inv_scale.reshape(1, -1),
        task_mix.T,
        task_diag.reshape(1, -1),
        task_noise.reshape(1, -1),
    )
    groups = [
        [(2 * y + c) * n_col + n_z * x + z for y in range(n_y) for z in range(n_z)]
        for c in range(2)
        for x in range(n_x)
    ]
    cols = lax.all_to_all(
        cols, axes, split_axis=0, concat_axis=0, tiled=True, axis_index_groups=groups
    )

    def along_x(value, k):
        return lax.ppermute(value, "col", [(i, (i + n_z * k) % n_col) for i in range(n_col)])

    def other_core(value):
        return lax.ppermute(value, "row", [(i, i ^ 1) for i in range(n_row)])

    own_core = [share] + [along_x(share, k) for k in range(1, n_x)]
    near, far = product_call(table, cols, own_core + [other_core(c) for c in own_core])
    sums = pl.pallas_call(
        add_kernel,
        in_specs=[VMEM] * 2,
        out_specs=[VMEM] * n_x,
        out_shape=[shape] * n_x,
        compiler_params=PARAMS,
        name="add",
    )(near, other_core(far))
    parts = [sums[0]] + [along_x(sums[k], -k) for k in range(1, n_x)]
    send = pl.pallas_call(
        image_kernel,
        in_specs=[VMEM] * (3 + n_x),
        out_specs=VMEM,
        out_shape=jax.ShapeDtypeStruct((devices, 3, 128), F32),
        compiler_params=PARAMS,
        name="image",
    )(nv, vq, pos, *parts)
    got = lax.all_to_all(send, ("row", "col"), split_axis=0, concat_axis=0, tiled=True)
    residual, direction, alpha, beta = pl.pallas_call(
        final_kernel,
        in_specs=[VMEM],
        out_specs=[VMEM] * 4,
        out_shape=[
            jax.ShapeDtypeStruct((width, rows), F32),
            jax.ShapeDtypeStruct((width, rows), F32),
            jax.ShapeDtypeStruct((1, width), F32),
            jax.ShapeDtypeStruct((1, width), F32),
        ],
        compiler_params=PARAMS,
        name="final",
    )(got)
    return residual.T, direction.T, alpha.reshape(width), beta.reshape(width)


def solution(mesh):
    axes = ("row", "col")
    return jax.shard_map(
        body,
        mesh=mesh,
        in_specs=(
            P(axes, None),
            P(axes),
            P(),
            P(axes),
            P(axes, None),
            P(),
            P(),
            P(),
            P(),
            P(),
            P(),
        ),
        out_specs=(P(axes, None), P(axes, None), P(), P()),
        check_vma=False,
    )
```

```python
import functools
import math

import jax
import jax.numpy as jnp
from jax import lax
from jax.experimental import pallas as pl
from jax.experimental.pallas import tpu as pltpu
from jax.sharding import PartitionSpec as P

F32 = jnp.float32
BF16 = jnp.bfloat16
VMEM = pl.BlockSpec(memory_space=pltpu.VMEM)
SMEM = pl.BlockSpec(memory_space=pltpu.SMEM)
PARAMS = pltpu.CompilerParams(vmem_limit_bytes=16 * 1024 * 1024)
ALONE = pltpu.CompilerParams(vmem_limit_bytes=60 * 1024 * 1024)
LARGE = pltpu.CompilerParams(vmem_limit_bytes=36 * 1024 * 1024)
V0, T0, N0, ONE, P0, S0 = 64, 96, 97, 100, 103, 112
LOG2E = math.log2(math.e)


def iota(shape, dim):
    return lax.broadcasted_iota(jnp.int32, shape, dim)


def split3(x):
    hi = x.astype(BF16)
    rest = x - hi.astype(F32)
    mid = rest.astype(BF16)
    low = (rest - mid.astype(F32)).astype(BF16)
    return hi, mid, low


def look_up(table, task):
    hit = (iota((table.shape[1], task.shape[1]), 0) == task).astype(BF16)
    tab = jnp.concatenate(split3(table), axis=0)
    got = jnp.dot(tab, hit, preferred_element_type=F32)
    return got[0:8] + got[8:16] + got[16:24]


def order_of(tid, cnt, rank):
    rows, ntask = tid.shape[1], cnt.shape[1]
    counts = cnt[...].astype(F32)
    before = iota((ntask, ntask), 1) < iota((ntask, ntask), 0)
    start = jnp.sum(jnp.where(before, counts, 0.0), axis=1, keepdims=True)
    hit = iota((ntask, rows), 0) == tid[...]
    pos = jnp.sum(jnp.where(hit, start, 0.0), axis=0, keepdims=True) + rank[...].astype(F32)
    pos_col = jnp.concatenate([pos, jnp.zeros((7, rows), F32)], axis=0).T[:, 0:1]
    return pos, jnp.sum((pos_col < pos).astype(F32), axis=0, keepdims=True)


def pack_kernel(
    feat, tid, cnt, rank, probes, net_w, net_b, scale, mix, diag, noise_in,
    cols, rows_out, vq_out, nv_out, pos_out, table_out,
):
    rows = feat.shape[1]
    width = probes.shape[0]
    pos, order = order_of(tid, cnt, rank)
    task = tid[...]
    table = jnp.concatenate(
        [mix[...], diag[...], noise_in[...], jnp.zeros((2, mix.shape[1]), F32)], axis=0
    )
    table_out[...] = table
    column = jnp.concatenate([net_b[...], scale[...], jnp.zeros((6, 64), F32)], axis=0).T
    hidden = jnp.tanh(
        lax.dot_general(
            net_w[...], feat[...], (((0,), (0,)), ((), ())), preferred_element_type=F32
        )
        + column[:, 0:1]
    )
    latent = (hidden * column[:, 1:2]).astype(BF16)
    lat = latent.astype(F32)
    norm = jnp.sum(lat * lat, axis=0, keepdims=True) * (-0.5 * LOG2E)
    local = pos - jnp.floor(pos * (1.0 / rows)) * rows
    high = jnp.floor(local * (1.0 / 16.0))
    noise = look_up(table, task)[5:6]
    extra = jnp.concatenate(
        [task.astype(F32)]
        + [a.astype(F32) for a in split3(norm)]
        + [jnp.ones((3, rows), F32), high, local - 16.0 * high, jnp.zeros((7, rows), F32)]
        + [a.astype(F32) for a in split3(noise)]
        + [jnp.zeros((13, rows), F32)],
        axis=0,
    ).astype(BF16)
    whole = jnp.concatenate([latent, probes[...], extra], axis=0)
    tile = jnp.floor(order * (1.0 / 64.0))
    inner = order - tile * 64.0
    block = jnp.floor(inner * 0.25)
    order_r = tile * 64.0 + (inner - block * 4.0) * 16.0 + block
    square = iota((rows, rows), 0)
    place_c = (square == order.astype(jnp.int32)).astype(BF16)
    place_r = (square == order_r.astype(jnp.int32)).astype(BF16)
    turn = (((1,), (1,)), ((), ()))
    data = lax.dot_general(place_c, whole, turn, preferred_element_type=F32).astype(BF16)
    cols[...] = data
    data = lax.dot_general(place_r, whole, turn, preferred_element_type=F32)
    half = rows // 2
    pair = jnp.concatenate([data[:half, :V0], data[half:, :V0]], axis=1).astype(BF16)
    at = (iota((16, rows), 1) % 16 == iota((16, rows), 0)).astype(BF16)
    group = jnp.where(iota((rows, 128), 0) // 16 == iota((rows, 128), 1), data[:, T0 : T0 + 1], 0.0)
    tasks = jnp.dot(at, group.astype(BF16), preferred_element_type=F32).astype(BF16)
    for k in range(rows_out.shape[0]):
        rows_out[k, :half, :] = pair
        rows_out[k, half:, :] = tasks
    place = data[:, P0 : P0 + 1] * 16.0 + data[:, P0 + 1 : P0 + 2]
    noise_c = data[:, S0 : S0 + 1] + data[:, S0 + 1 : S0 + 2] + data[:, S0 + 2 : S0 + 3]
    v = data[:, V0:T0]
    nv = noise_c * v

    def fold(x, m):
        return jnp.concatenate(
            [x[t * 64 + m * 16 : t * 64 + m * 16 + 16] for t in range(rows // 64)], axis=0
        )

    vq_out[...] = jnp.concatenate([fold(v, m) for m in range(4)], axis=1)
    nv_out[...] = jnp.concatenate([fold(nv, m) for m in range(4)], axis=1)
    lane = iota((rows // 4, 128), 1)
    posq = jnp.zeros((rows // 4, 128), F32)
    for m in range(4):
        posq = jnp.where(lane == 3 * width + m, fold(place, m), posq)
    pos_out[...] = posq


def prepare_cols(table, cols, zc, st):
    rows = cols[0].shape[0]
    size = 4 * 16 * len(cols)
    width = T0 - V0
    for k in range(rows // 64):
        data = jnp.concatenate(
            [c[g * 16 : g * 16 + 16, :] for g in range(4 * k, 4 * k + 4) for c in cols],
            axis=0,
        )
        span = slice(k * size, (k + 1) * size)
        wide = data.astype(F32)
        zc[span, 128:] = data
        zc[span, :128] = jnp.where(iota((size, 128), 1) < V0, wide, pltpu.roll(wide, V0, 1)).astype(BF16)
        turned = wide.T
        weight = look_up(table, turned[T0 : T0 + 1].astype(jnp.int32))
        values = turned[V0:T0]
        for q in range(4):
            st[q * width : (q + 1) * width, span] = (weight[q : q + 1] * values).astype(BF16)
        st[4 * width :, span] = values.astype(BF16)


def product_kernel(tile, own_col, table, gathered, *refs):
    cols, (out, own, kern_ref, task_ref, zc, st, mine) = refs[:-7], refs[-7:]
    t = pl.program_id(0)
    steps = pl.num_programs(0)
    n_col = gathered.shape[0]
    half = gathered.shape[1] - 16
    wide = n_col * 16
    rows = 4 * wide
    tab = table[...]

    @pl.when(t == 0)
    def _():
        every = gathered[:, half:, :].reshape(wide, 128).astype(F32).T
        for k in range(task_ref.shape[0]):
            task_ref[k] = every[4 * k : 4 * k + 8]
        prepare_cols(tab, cols, zc, st)

    first = pl.multiple_of(lax.rem(t, steps // 2) * 64, 64)
    blocks = [gathered[k, pl.ds(first, 64), :] for k in range(n_col)]
    data = jnp.concatenate(
        [b[m * 16 : m * 16 + 16, :] for m in range(4) for b in blocks], axis=0
    )
    turned = data.astype(F32).T
    z = jnp.where(t < steps // 2, turned[:V0], turned[V0:])
    norm = jnp.sum(z * z, axis=0, keepdims=True) * (-0.5 * LOG2E)
    parts = [a.astype(F32) for a in split3(norm)]
    sub = iota((T0 - V0, rows), 0)
    extra = jnp.where(jnp.logical_and(sub >= N0 - T0, sub < ONE - T0), 1.0, 0.0)
    for k in range(3):
        extra = jnp.where(sub == ONE - T0 + k, parts[k], extra)
    z = jnp.concatenate(
        split3(z * LOG2E) + (jnp.zeros((T0 - V0, rows), BF16), extra.astype(BF16)), axis=0
    )
    four = task_ref[t]
    task = jnp.concatenate([four[m : m + 1] for m in range(4)], axis=1)
    weight = look_up(tab, task.astype(jnp.int32))
    width = st.shape[0] // 5
    total = None
    for j in range(zc.shape[0] // tile):
        span = slice(j * tile, (j + 1) * tile)
        x = jnp.dot(zc[span, :], z, preferred_element_type=F32)
        kern = jnp.minimum(jnp.exp2(x).astype(BF16), jnp.asarray(1.0, BF16))
        kern_ref[span, :] = kern
        part = jnp.dot(st[: 4 * width, span], kern, preferred_element_type=F32)
        total = part if total is None else total + part
    size = zc.shape[0] // 32
    band = pl.ds(pl.multiple_of(jnp.clip(4 * t - 1, 0, 26) * size, size), 6 * size)
    same = zc[band, 128 + T0 : 129 + T0] == task.astype(BF16)
    kept = jnp.where(same, kern_ref[band, :], jnp.asarray(0.0, BF16))
    summed = weight[4:5] * jnp.dot(st[4 * width :, band], kept, preferred_element_type=F32)
    for q in range(4):
        summed = summed + weight[q : q + 1] * total[q * width : (q + 1) * width]
    folded = jnp.concatenate(
        [summed[:, m * wide : (m + 1) * wide] for m in range(4)], axis=0
    ).T.reshape(n_col, 16, 128)
    out[...] = folded.astype(out.dtype)
    mine[...] = folded
    own[...] = mine[own_col[0]]


def product_call(col, table, gathered, cols):
    n_col, packed, _ = gathered.shape
    total = len(cols) * cols[0].shape[0]
    tiles = (packed - 16) // 32
    rows = n_col * 64
    return pl.pallas_call(
        functools.partial(product_kernel, 2048),
        grid=(tiles,),
        in_specs=[SMEM] + [VMEM] * (2 + len(cols)),
        out_specs=[
            pl.BlockSpec((n_col, 16, 128), lambda i: (0, i, 0)),
            pl.BlockSpec((16, 128), lambda i: (i, 0)),
        ],
        out_shape=[
            jax.ShapeDtypeStruct((n_col, tiles * 16, 128), BF16),
            jax.ShapeDtypeStruct((tiles * 16, 128), F32),
        ],
        scratch_shapes=[
            pltpu.VMEM((total, rows), BF16),
            pltpu.VMEM((tiles, 8, n_col * 16), F32),
            pltpu.VMEM((total, 256), BF16),
            pltpu.VMEM((5 * (T0 - V0), total), BF16),
            pltpu.VMEM((n_col, 16, 128), F32),
        ],
        compiler_params=LARGE,
        cost_estimate=pl.CostEstimate(
            flops=2 * tiles * rows * total * 512, bytes_accessed=4 << 20, transcendentals=0
        ),
        name="product",
    )(col, table, gathered, *cols)


def image_kernel(col, parts, own, vq, nv, pos, send):
    img = own[...] + nv[...]
    for k in range(parts.shape[0]):
        img = img + jnp.where(k == col[0], 0.0, parts[k].astype(F32))
    v = vq[...]

    def over(x):
        s = jnp.sum(x, axis=0, keepdims=True)
        return s[:, 0:32] + s[:, 32:64] + s[:, 64:96] + s[:, 96:128]

    vv, vi = over(v * v), over(v * img)
    ratio = jnp.where(vv > 0.0, vi / jnp.where(vv > 0.0, vv, 1.0), 0.0)
    rest = img - jnp.concatenate([ratio] * 4, axis=1) * v
    row = jnp.concatenate([vv, vi, over(rest * rest), jnp.zeros_like(vv)], axis=1)
    send[:, 0, :] = img
    send[:, 1, :] = v
    send[:, 2, :] = pos[...] + row


def final_kernel(got, residual, direction, alpha_out, beta_out):
    n = got.shape[0]
    rows = residual.shape[1]
    img, v, every = got[:, 0, :], got[:, 1, :], got[:, 2, :]
    vv, vi, rr = every[:, 0:32], every[:, 32:64], every[:, 64:96]
    total_v = jnp.sum(vv, axis=0, keepdims=True)
    total_i = jnp.sum(vi, axis=0, keepdims=True)
    center = total_i / total_v
    ratio = jnp.where(vv > 0.0, vi / jnp.where(vv > 0.0, vv, 1.0), 0.0)
    shift = ratio - center
    total_r = jnp.sum(rr + vv * (shift * shift), axis=0, keepdims=True)
    alpha = total_v / total_i
    beta = alpha * alpha * total_r / total_v
    alpha_out[...] = alpha
    beta_out[...] = beta
    res = v - jnp.concatenate([alpha] * 4, axis=1) * img
    pieces = split3(res) + (v.astype(BF16),)
    total = None
    for m in range(4):
        lanes = slice(m * 32, (m + 1) * 32)
        values = jnp.concatenate([p[:, lanes] for p in pieces], axis=1)
        place = every[:, 96 + m : 97 + m].astype(jnp.int32)
        onehot = (iota((n, rows), 1) == place).astype(BF16)
        part = lax.dot_general(
            values, onehot, (((0,), (0,)), ((), ())), preferred_element_type=F32
        )
        total = part if total is None else total + part
    res_t = total[0:32] + total[32:64] + total[64:96]
    residual[...] = res_t
    beta_col = jnp.concatenate([beta, jnp.zeros((7, 32), F32)], axis=0).T[:, 0:1]
    direction[...] = res_t + beta_col * total[96:128]


def body(
    features,
    task_id,
    task_count,
    task_rank,
    probes,
    net_w,
    net_b,
    inv_scale,
    task_mix,
    task_diag,
    task_noise,
):
    rows = features.shape[0]
    n_row, n_col = lax.axis_size("row"), lax.axis_size("col")
    devices = n_row * n_col
    axes = ("row", "col")
    width = probes.shape[1]
    quarter = rows // 4
    col = lax.axis_index("col").astype(jnp.int32).reshape(1)
    shape = jax.ShapeDtypeStruct((quarter, 128), F32)
    cols, share, vq, nv, pos, table = pl.pallas_call(
        pack_kernel,
        in_specs=[VMEM] * 11,
        out_specs=[VMEM] * 6,
        out_shape=[
            jax.ShapeDtypeStruct((rows, 128), BF16),
            jax.ShapeDtypeStruct((n_col, rows // 2 + 16, 128), BF16),
            shape,
            shape,
            shape,
            jax.ShapeDtypeStruct((8, task_count.shape[0]), F32),
        ],
        compiler_params=ALONE,
        name="pack",
    )(
        features.T,
        task_id.reshape(1, -1),
        task_count.reshape(1, -1),
        task_rank.reshape(1, -1),
        probes.T,
        net_w,
        net_b.reshape(1, -1),
        inv_scale.reshape(1, -1),
        task_mix.T,
        task_diag.reshape(1, -1),
        task_noise.reshape(1, -1),
    )
    gathered = lax.all_to_all(share, "col", split_axis=0, concat_axis=0, tiled=True)
    chunks = [cols] + [
        lax.ppermute(cols, "row", [(i, (i + 2 * k) % n_row) for i in range(n_row)])
        for k in range(1, n_row // 2)
    ]
    chunks = chunks + [lax.ppermute(c, "row", [(i, i ^ 1) for i in range(n_row)]) for c in chunks]
    parts, own = product_call(col, table, gathered, chunks)
    summed = lax.all_to_all(parts, "col", split_axis=0, concat_axis=0, tiled=True)
    send = pl.pallas_call(
        image_kernel,
        in_specs=[SMEM] + [VMEM] * 5,
        out_specs=VMEM,
        out_shape=jax.ShapeDtypeStruct((devices, 3, 128), F32),
        compiler_params=PARAMS,
        name="image",
    )(col, summed, own, vq, nv, pos)
    got = lax.all_to_all(send, ("row", "col"), split_axis=0, concat_axis=0, tiled=True)
    residual, direction, alpha, beta = pl.pallas_call(
        final_kernel,
        in_specs=[VMEM],
        out_specs=[VMEM] * 4,
        out_shape=[
            jax.ShapeDtypeStruct((width, rows), F32),
            jax.ShapeDtypeStruct((width, rows), F32),
            jax.ShapeDtypeStruct((1, width), F32),
            jax.ShapeDtypeStruct((1, width), F32),
        ],
        compiler_params=PARAMS,
        name="final",
    )(got)
    return residual.T, direction.T, alpha.reshape(width), beta.reshape(width)


def solution(mesh):
    axes = ("row", "col")
    return jax.shard_map(
        body,
        mesh=mesh,
        in_specs=(
            P(axes, None),
            P(axes),
            P(),
            P(axes),
            P(axes, None),
            P(),
            P(),
            P(),
            P(),
            P(),
            P(),
        ),
        out_specs=(P(axes, None), P(axes, None), P(), P()),
        check_vma=False,
    )
```

```python
import functools
import math

import jax
import jax.numpy as jnp
from jax import lax
from jax.experimental import pallas as pl
from jax.experimental.pallas import tpu as pltpu
from jax.sharding import PartitionSpec as P

F32 = jnp.float32
BF16 = jnp.bfloat16
VMEM = pl.BlockSpec(memory_space=pltpu.VMEM)
SMEM = pl.BlockSpec(memory_space=pltpu.SMEM)
PARAMS = pltpu.CompilerParams(vmem_limit_bytes=16 * 1024 * 1024)
ALONE = pltpu.CompilerParams(vmem_limit_bytes=60 * 1024 * 1024)
LARGE = pltpu.CompilerParams(vmem_limit_bytes=36 * 1024 * 1024)
V0, T0, N0, ONE, P0, S0 = 64, 96, 97, 100, 103, 112
LOG2E = math.log2(math.e)


def iota(shape, dim):
    return lax.broadcasted_iota(jnp.int32, shape, dim)


def split3(x):
    hi = x.astype(BF16)
    rest = x - hi.astype(F32)
    mid = rest.astype(BF16)
    low = (rest - mid.astype(F32)).astype(BF16)
    return hi, mid, low


def look_up(table, task):
    hit = (iota((table.shape[1], task.shape[1]), 0) == task).astype(BF16)
    tab = jnp.concatenate(split3(table), axis=0)
    got = jnp.dot(tab, hit, preferred_element_type=F32)
    return got[0:8] + got[8:16] + got[16:24]


def order_of(tid, cnt, rank):
    rows, ntask = tid.shape[1], cnt.shape[1]
    counts = cnt[...].astype(F32)
    before = iota((ntask, ntask), 1) < iota((ntask, ntask), 0)
    start = jnp.sum(jnp.where(before, counts, 0.0), axis=1, keepdims=True)
    hit = iota((ntask, rows), 0) == tid[...]
    pos = jnp.sum(jnp.where(hit, start, 0.0), axis=0, keepdims=True) + rank[...].astype(F32)
    pos_col = jnp.concatenate([pos, jnp.zeros((7, rows), F32)], axis=0).T[:, 0:1]
    return pos, jnp.sum((pos_col < pos).astype(F32), axis=0, keepdims=True)


def pack_kernel(
    feat, tid, cnt, rank, probes, net_w, net_b, scale, mix, diag, noise_in,
    cols, rows_out, vq_out, nv_out, pos_out, table_out,
):
    rows = feat.shape[1]
    width = probes.shape[0]
    pos, order = order_of(tid, cnt, rank)
    task = tid[...]
    table = jnp.concatenate(
        [mix[...], diag[...], noise_in[...], jnp.zeros((2, mix.shape[1]), F32)], axis=0
    )
    table_out[...] = table
    column = jnp.concatenate([net_b[...], scale[...], jnp.zeros((6, 64), F32)], axis=0).T
    hidden = jnp.tanh(
        lax.dot_general(
            net_w[...], feat[...], (((0,), (0,)), ((), ())), preferred_element_type=F32
        )
        + column[:, 0:1]
    )
    latent = (hidden * column[:, 1:2]).astype(BF16)
    lat = latent.astype(F32)
    norm = jnp.sum(lat * lat, axis=0, keepdims=True) * (-0.5 * LOG2E)
    local = pos - jnp.floor(pos * (1.0 / rows)) * rows
    high = jnp.floor(local * (1.0 / 16.0))
    noise = look_up(table, task)[5:6]
    extra = jnp.concatenate(
        [task.astype(F32)]
        + [a.astype(F32) for a in split3(norm)]
        + [jnp.ones((3, rows), F32), high, local - 16.0 * high, jnp.zeros((7, rows), F32)]
        + [a.astype(F32) for a in split3(noise)]
        + [jnp.zeros((13, rows), F32)],
        axis=0,
    ).astype(BF16)
    whole = jnp.concatenate([latent, probes[...], extra], axis=0)
    tile = jnp.floor(order * (1.0 / 64.0))
    inner = order - tile * 64.0
    block = jnp.floor(inner * 0.25)
    order_r = tile * 64.0 + (inner - block * 4.0) * 16.0 + block
    square = iota((rows, rows), 0)
    place_c = (square == order.astype(jnp.int32)).astype(BF16)
    place_r = (square == order_r.astype(jnp.int32)).astype(BF16)
    turn = (((1,), (1,)), ((), ()))
    data = lax.dot_general(place_c, whole, turn, preferred_element_type=F32).astype(BF16)
    cols[...] = data
    data = lax.dot_general(place_r, whole, turn, preferred_element_type=F32)
    half = rows // 2
    pair = jnp.concatenate([data[:half, :V0], data[half:, :V0]], axis=1).astype(BF16)
    at = (iota((16, rows), 1) % 16 == iota((16, rows), 0)).astype(BF16)
    group = jnp.where(iota((rows, 128), 0) // 16 == iota((rows, 128), 1), data[:, T0 : T0 + 1], 0.0)
    tasks = jnp.dot(at, group.astype(BF16), preferred_element_type=F32).astype(BF16)
    for k in range(rows_out.shape[0]):
        rows_out[k, :half, :] = pair
        rows_out[k, half:, :] = tasks
    place = data[:, P0 : P0 + 1] * 16.0 + data[:, P0 + 1 : P0 + 2]
    noise_c = data[:, S0 : S0 + 1] + data[:, S0 + 1 : S0 + 2] + data[:, S0 + 2 : S0 + 3]
    v = data[:, V0:T0]
    nv = noise_c * v

    def fold(x, m):
        return jnp.concatenate(
            [x[t * 64 + m * 16 : t * 64 + m * 16 + 16] for t in range(rows // 64)], axis=0
        )

    vq_out[...] = jnp.concatenate([fold(v, m) for m in range(4)], axis=1)
    nv_out[...] = jnp.concatenate([fold(nv, m) for m in range(4)], axis=1)
    lane = iota((rows // 4, 128), 1)
    posq = jnp.zeros((rows // 4, 128), F32)
    for m in range(4):
        posq = jnp.where(lane == 3 * width + m, fold(place, m), posq)
    pos_out[...] = posq


def prepare_cols(table, cols, zc, st):
    rows = cols[0].shape[0]
    size = 4 * 16 * len(cols)
    width = T0 - V0
    for k in range(rows // 64):
        data = jnp.concatenate(
            [c[g * 16 : g * 16 + 16, :] for g in range(4 * k, 4 * k + 4) for c in cols],
            axis=0,
        )
        span = slice(k * size, (k + 1) * size)
        wide = data.astype(F32)
        zc[span, 128:] = data
        zc[span, :128] = jnp.where(iota((size, 128), 1) < V0, wide, pltpu.roll(wide, V0, 1)).astype(BF16)
        turned = wide.T
        weight = look_up(table, turned[T0 : T0 + 1].astype(jnp.int32))
        values = turned[V0:T0]
        for q in range(4):
            st[q * width : (q + 1) * width, span] = (weight[q : q + 1] * values).astype(BF16)
        st[4 * width :, span] = values.astype(BF16)


def product_kernel(tile, own_col, table, gathered, *refs):
    cols, (out, own, kern_ref, task_ref, zc, st, mine) = refs[:-7], refs[-7:]
    t = pl.program_id(0)
    steps = pl.num_programs(0)
    n_col = gathered.shape[0]
    half = gathered.shape[1] - 16
    wide = n_col * 16
    rows = 4 * wide
    tab = table[...]

    @pl.when(t == 0)
    def _():
        every = gathered[:, half:, :].reshape(wide, 128).astype(F32).T
        for k in range(task_ref.shape[0]):
            task_ref[k] = every[4 * k : 4 * k + 8]
        prepare_cols(tab, cols, zc, st)

    first = pl.multiple_of(lax.rem(t, steps // 2) * 64, 64)
    blocks = [gathered[k, pl.ds(first, 64), :] for k in range(n_col)]
    data = jnp.concatenate(
        [b[m * 16 : m * 16 + 16, :] for m in range(4) for b in blocks], axis=0
    )
    turned = data.astype(F32).T
    z = jnp.where(t < steps // 2, turned[:V0], turned[V0:])
    norm = jnp.sum(z * z, axis=0, keepdims=True) * (-0.5 * LOG2E)
    parts = [a.astype(F32) for a in split3(norm)]
    sub = iota((T0 - V0, rows), 0)
    extra = jnp.where(jnp.logical_and(sub >= N0 - T0, sub < ONE - T0), 1.0, 0.0)
    for k in range(3):
        extra = jnp.where(sub == ONE - T0 + k, parts[k], extra)
    z = jnp.concatenate(
        split3(z * LOG2E) + (jnp.zeros((T0 - V0, rows), BF16), extra.astype(BF16)), axis=0
    )
    four = task_ref[t]
    task = jnp.concatenate([four[m : m + 1] for m in range(4)], axis=1)
    weight = look_up(tab, task.astype(jnp.int32))
    width = st.shape[0] // 5
    total = None
    for j in range(zc.shape[0] // tile):
        span = slice(j * tile, (j + 1) * tile)
        x = jnp.dot(zc[span, :], z, preferred_element_type=F32)
        kern = jnp.minimum(jnp.exp2(x).astype(BF16), jnp.asarray(1.0, BF16))
        kern_ref[span, :] = kern
        part = jnp.dot(st[: 4 * width, span], kern, preferred_element_type=F32)
        total = part if total is None else total + part
    size = zc.shape[0] // 32
    band = pl.ds(pl.multiple_of(jnp.clip(4 * t - 1, 0, 26) * size, size), 6 * size)
    same = zc[band, 128 + T0 : 129 + T0] == task.astype(BF16)
    kept = jnp.where(same, kern_ref[band, :], jnp.asarray(0.0, BF16))
    summed = weight[4:5] * jnp.dot(st[4 * width :, band], kept, preferred_element_type=F32)
    for q in range(4):
        summed = summed + weight[q : q + 1] * total[q * width : (q + 1) * width]
    folded = jnp.concatenate(
        [summed[:, m * wide : (m + 1) * wide] for m in range(4)], axis=0
    ).T.reshape(n_col, 16, 128)
    out[...] = folded.astype(out.dtype)
    mine[...] = folded
    own[...] = mine[own_col[0]]


def product_call(col, table, gathered, cols):
    n_col, packed, _ = gathered.shape
    total = len(cols) * cols[0].shape[0]
    tiles = (packed - 16) // 32
    rows = n_col * 64
    return pl.pallas_call(
        functools.partial(product_kernel, 2048),
        grid=(tiles,),
        in_specs=[SMEM] + [VMEM] * (2 + len(cols)),
        out_specs=[
            pl.BlockSpec((n_col, 16, 128), lambda i: (0, i, 0)),
            pl.BlockSpec((16, 128), lambda i: (i, 0)),
        ],
        out_shape=[
            jax.ShapeDtypeStruct((n_col, tiles * 16, 128), BF16),
            jax.ShapeDtypeStruct((tiles * 16, 128), F32),
        ],
        scratch_shapes=[
            pltpu.VMEM((total, rows), BF16),
            pltpu.VMEM((tiles, 8, n_col * 16), F32),
            pltpu.VMEM((total, 256), BF16),
            pltpu.VMEM((5 * (T0 - V0), total), BF16),
            pltpu.VMEM((n_col, 16, 128), F32),
        ],
        compiler_params=LARGE,
        cost_estimate=pl.CostEstimate(
            flops=2 * tiles * rows * total * 512, bytes_accessed=4 << 20, transcendentals=0
        ),
        name="product",
    )(col, table, gathered, *cols)


def image_kernel(col, parts, own, vq, nv, pos, send):
    img = own[...] + nv[...]
    for k in range(parts.shape[0]):
        img = img + jnp.where(k == col[0], 0.0, parts[k].astype(F32))
    v = vq[...]

    def over(x):
        s = jnp.sum(x, axis=0, keepdims=True)
        return s[:, 0:32] + s[:, 32:64] + s[:, 64:96] + s[:, 96:128]

    vv, vi = over(v * v), over(v * img)
    ratio = jnp.where(vv > 0.0, vi / jnp.where(vv > 0.0, vv, 1.0), 0.0)
    rest = img - jnp.concatenate([ratio] * 4, axis=1) * v
    row = jnp.concatenate([vv, vi, over(rest * rest), jnp.zeros_like(vv)], axis=1)
    send[:, 0, :] = img
    send[:, 1, :] = v
    send[:, 2, :] = pos[...] + row


def final_kernel(got, residual, direction, alpha_out, beta_out):
    n = got.shape[0]
    rows = residual.shape[1]
    every = got[:, 2, :]
    turned = every.T

    def over(axis, pick):
        vv, vi, rr = (pick(k) for k in range(3))
        total_v = jnp.sum(vv, axis=axis, keepdims=True)
        total_i = jnp.sum(vi, axis=axis, keepdims=True)
        ratio = jnp.where(vv > 0.0, vi / jnp.where(vv > 0.0, vv, 1.0), 0.0)
        shift = ratio - total_i / total_v
        total_r = jnp.sum(rr + vv * (shift * shift), axis=axis, keepdims=True)
        alpha = total_v / total_i
        return alpha, alpha * alpha * total_r / total_v

    alpha, beta = over(1, lambda k: turned[32 * k : 32 * k + 32])
    sums = jnp.concatenate([alpha, beta, jnp.zeros((32, 126), F32)], axis=1).T
    alpha_out[...] = sums[0:1]
    beta_out[...] = sums[1:2]
    v = got[:, 1, :].T
    res = v - jnp.concatenate([alpha] * 4, axis=0) * got[:, 0, :].T
    pieces = split3(res) + (v.astype(BF16),)
    total = None
    for m in range(4):
        lanes = slice(m * 32, (m + 1) * 32)
        values = jnp.concatenate([p[lanes] for p in pieces], axis=0)
        place = every[:, 96 + m : 97 + m].astype(jnp.int32)
        onehot = (iota((n, rows), 1) == place).astype(BF16)
        part = jnp.dot(values, onehot, preferred_element_type=F32)
        total = part if total is None else total + part
    res_t = total[0:32] + total[32:64] + total[64:96]
    residual[...] = res_t
    direction[...] = res_t + beta * total[96:128]


def body(
    features,
    task_id,
    task_count,
    task_rank,
    probes,
    net_w,
    net_b,
    inv_scale,
    task_mix,
    task_diag,
    task_noise,
):
    rows = features.shape[0]
    n_row, n_col = lax.axis_size("row"), lax.axis_size("col")
    devices = n_row * n_col
    axes = ("row", "col")
    width = probes.shape[1]
    quarter = rows // 4
    col = lax.axis_index("col").astype(jnp.int32).reshape(1)
    shape = jax.ShapeDtypeStruct((quarter, 128), F32)
    cols, share, vq, nv, pos, table = pl.pallas_call(
        pack_kernel,
        in_specs=[VMEM] * 11,
        out_specs=[VMEM] * 6,
        out_shape=[
            jax.ShapeDtypeStruct((rows, 128), BF16),
            jax.ShapeDtypeStruct((n_col, rows // 2 + 16, 128), BF16),
            shape,
            shape,
            shape,
            jax.ShapeDtypeStruct((8, task_count.shape[0]), F32),
        ],
        compiler_params=ALONE,
        name="pack",
    )(
        features.T,
        task_id.reshape(1, -1),
        task_count.reshape(1, -1),
        task_rank.reshape(1, -1),
        probes.T,
        net_w,
        net_b.reshape(1, -1),
        inv_scale.reshape(1, -1),
        task_mix.T,
        task_diag.reshape(1, -1),
        task_noise.reshape(1, -1),
    )
    gathered = lax.all_to_all(share, "col", split_axis=0, concat_axis=0, tiled=True)
    chunks = [cols] + [
        lax.ppermute(cols, "row", [(i, (i + 2 * k) % n_row) for i in range(n_row)])
        for k in range(1, n_row // 2)
    ]
    chunks = chunks + [lax.ppermute(c, "row", [(i, i ^ 1) for i in range(n_row)]) for c in chunks]
    parts, own = product_call(col, table, gathered, chunks)
    summed = lax.all_to_all(parts, "col", split_axis=0, concat_axis=0, tiled=True)
    send = pl.pallas_call(
        image_kernel,
        in_specs=[SMEM] + [VMEM] * 5,
        out_specs=VMEM,
        out_shape=jax.ShapeDtypeStruct((devices, 3, 128), F32),
        compiler_params=PARAMS,
        name="image",
    )(col, summed, own, vq, nv, pos)
    got = lax.all_to_all(send, ("row", "col"), split_axis=0, concat_axis=0, tiled=True)
    residual, direction, alpha, beta = pl.pallas_call(
        final_kernel,
        in_specs=[VMEM],
        out_specs=[VMEM] * 4,
        out_shape=[
            jax.ShapeDtypeStruct((width, rows), F32),
            jax.ShapeDtypeStruct((width, rows), F32),
            jax.ShapeDtypeStruct((1, width), F32),
            jax.ShapeDtypeStruct((1, width), F32),
        ],
        compiler_params=PARAMS,
        name="final",
    )(got)
    return residual.T, direction.T, alpha.reshape(width), beta.reshape(width)


def solution(mesh):
    axes = ("row", "col")
    return jax.shard_map(
        body,
        mesh=mesh,
        in_specs=(
            P(axes, None),
            P(axes),
            P(),
            P(axes),
            P(axes, None),
            P(),
            P(),
            P(),
            P(),
            P(),
            P(),
        ),
        out_specs=(P(axes, None), P(axes, None), P(), P()),
        check_vma=False,
    )
```

```python
import functools
import math

import jax
import jax.numpy as jnp
from jax import lax
from jax.experimental import pallas as pl
from jax.experimental.pallas import tpu as pltpu
from jax.sharding import PartitionSpec as P

F32 = jnp.float32
BF16 = jnp.bfloat16
VMEM = pl.BlockSpec(memory_space=pltpu.VMEM)
SMEM = pl.BlockSpec(memory_space=pltpu.SMEM)
PARAMS = pltpu.CompilerParams(vmem_limit_bytes=16 * 1024 * 1024)
ALONE = pltpu.CompilerParams(vmem_limit_bytes=60 * 1024 * 1024)
LARGE = pltpu.CompilerParams(vmem_limit_bytes=36 * 1024 * 1024)
V0, T0, N0, ONE, P0, S0 = 64, 96, 97, 100, 103, 112
LOG2E = math.log2(math.e)


def iota(shape, dim):
    return lax.broadcasted_iota(jnp.int32, shape, dim)


def split3(x):
    hi = x.astype(BF16)
    rest = x - hi.astype(F32)
    mid = rest.astype(BF16)
    low = (rest - mid.astype(F32)).astype(BF16)
    return hi, mid, low


def look_up(table, task):
    hit = (iota((table.shape[1], task.shape[1]), 0) == task).astype(BF16)
    tab = jnp.concatenate(split3(table), axis=0)
    got = jnp.dot(tab, hit, preferred_element_type=F32)
    return got[0:8] + got[8:16] + got[16:24]


def order_of(tid, cnt, rank):
    rows, ntask = tid.shape[1], cnt.shape[1]
    counts = cnt[...].astype(F32)
    before = iota((ntask, ntask), 1) < iota((ntask, ntask), 0)
    start = jnp.sum(jnp.where(before, counts, 0.0), axis=1, keepdims=True)
    hit = iota((ntask, rows), 0) == tid[...]
    pos = jnp.sum(jnp.where(hit, start, 0.0), axis=0, keepdims=True) + rank[...].astype(F32)
    pos_col = jnp.concatenate([pos, jnp.zeros((7, rows), F32)], axis=0).T[:, 0:1]
    return pos, jnp.sum((pos_col < pos).astype(F32), axis=0, keepdims=True)


def pack_kernel(
    feat, tid, cnt, rank, probes, net_w, net_b, scale, mix, diag, noise_in,
    cols, rows_out, vq_out, nv_out, pos_out, table_out,
):
    rows = feat.shape[1]
    width = probes.shape[0]
    pos, order = order_of(tid, cnt, rank)
    task = tid[...]
    table = jnp.concatenate(
        [mix[...], diag[...], noise_in[...], jnp.zeros((2, mix.shape[1]), F32)], axis=0
    )
    table_out[...] = table
    column = jnp.concatenate([net_b[...], scale[...], jnp.zeros((6, 64), F32)], axis=0).T
    hidden = jnp.tanh(
        lax.dot_general(
            net_w[...], feat[...], (((0,), (0,)), ((), ())), preferred_element_type=F32
        )
        + column[:, 0:1]
    )
    latent = (hidden * column[:, 1:2]).astype(BF16)
    lat = latent.astype(F32)
    norm = jnp.sum(lat * lat, axis=0, keepdims=True) * (-0.5 * LOG2E)
    local = pos - jnp.floor(pos * (1.0 / rows)) * rows
    high = jnp.floor(local * (1.0 / 16.0))
    noise = look_up(table, task)[5:6]
    extra = jnp.concatenate(
        [task.astype(F32)]
        + [a.astype(F32) for a in split3(norm)]
        + [jnp.ones((3, rows), F32), high, local - 16.0 * high, jnp.zeros((7, rows), F32)]
        + [a.astype(F32) for a in split3(noise)]
        + [jnp.zeros((13, rows), F32)],
        axis=0,
    ).astype(BF16)
    whole = jnp.concatenate([latent, probes[...], extra], axis=0)
    tile = jnp.floor(order * (1.0 / 64.0))
    inner = order - tile * 64.0
    block = jnp.floor(inner * 0.25)
    order_r = tile * 64.0 + (inner - block * 4.0) * 16.0 + block
    square = iota((rows, rows), 0)
    place_c = (square == order.astype(jnp.int32)).astype(BF16)
    place_r = (square == order_r.astype(jnp.int32)).astype(BF16)
    turn = (((1,), (1,)), ((), ()))
    data = lax.dot_general(place_c, whole, turn, preferred_element_type=F32).astype(BF16)
    cols[...] = data
    data = lax.dot_general(place_r, whole, turn, preferred_element_type=F32)
    half = rows // 2
    pair = jnp.concatenate([data[:half, :V0], data[half:, :V0]], axis=1).astype(BF16)
    at = (iota((16, rows), 1) % 16 == iota((16, rows), 0)).astype(BF16)
    group = jnp.where(iota((rows, 128), 0) // 16 == iota((rows, 128), 1), data[:, T0 : T0 + 1], 0.0)
    tasks = jnp.dot(at, group.astype(BF16), preferred_element_type=F32).astype(BF16)
    for k in range(rows_out.shape[0]):
        rows_out[k, :half, :] = pair
        rows_out[k, half:, :] = tasks
    place = data[:, P0 : P0 + 1] * 16.0 + data[:, P0 + 1 : P0 + 2]
    noise_c = data[:, S0 : S0 + 1] + data[:, S0 + 1 : S0 + 2] + data[:, S0 + 2 : S0 + 3]
    v = data[:, V0:T0]
    nv = noise_c * v

    def fold(x, m):
        return jnp.concatenate(
            [x[t * 64 + m * 16 : t * 64 + m * 16 + 16] for t in range(rows // 64)], axis=0
        )

    vq_out[...] = jnp.concatenate([fold(v, m) for m in range(4)], axis=1)
    nv_out[...] = jnp.concatenate([fold(nv, m) for m in range(4)], axis=1)
    lane = iota((rows // 4, 128), 1)
    posq = jnp.zeros((rows // 4, 128), F32)
    for m in range(4):
        posq = jnp.where(lane == 3 * width + m, fold(place, m), posq)
    pos_out[...] = posq


def prepare_cols(table, cols, zc, st):
    chunks = []
    for c in cols:
        chunks += [c] if len(c.shape) == 2 else [c.at[h] for h in range(c.shape[0])]
    rows = chunks[0].shape[0]
    size = 4 * 16 * len(chunks)
    width = T0 - V0
    for k in range(rows // 64):
        data = jnp.concatenate(
            [c[g * 16 : g * 16 + 16, :] for g in range(4 * k, 4 * k + 4) for c in chunks],
            axis=0,
        )
        span = slice(k * size, (k + 1) * size)
        wide = data.astype(F32)
        zc[span, 128:] = data
        zc[span, :128] = jnp.where(iota((size, 128), 1) < V0, wide, pltpu.roll(wide, V0, 1)).astype(BF16)
        turned = wide.T
        weight = look_up(table, turned[T0 : T0 + 1].astype(jnp.int32))
        values = turned[V0:T0]
        for q in range(4):
            st[q * width : (q + 1) * width, span] = (weight[q : q + 1] * values).astype(BF16)
        st[4 * width :, span] = values.astype(BF16)


def product_kernel(tile, pieces, last, own_chunk, table, gathered, *refs):
    cols, refs = refs[:pieces], refs[pieces:]
    if last:
        before, out, own, kern_ref, task_ref, zc, st, mine = refs
    else:
        out, kern_ref, task_ref, zc, st = refs
    i = pl.program_id(0)
    steps = pl.num_programs(0)
    chunks = gathered.shape[0]
    half = gathered.shape[1] - 16
    tab = table[...]

    @pl.when(i == 0)
    def _():
        every = gathered[:, half:, :].reshape(chunks * 16, 128).astype(F32).T
        for k in range(task_ref.shape[0]):
            task_ref[k] = every[8 * k : 8 * k + 8]
        prepare_cols(tab, cols, zc, st)

    first = pl.multiple_of(lax.rem(i, steps // 2) * 128, 128)
    blocks = [gathered[k, pl.ds(first, 128), :] for k in range(chunks)]
    data = jnp.concatenate(
        [b[g * 16 : g * 16 + 16, :] for g in range(8) for b in blocks], axis=0
    )
    rows = data.shape[0]
    turned = data.astype(F32).T
    z = jnp.where(i < steps // 2, turned[:V0], turned[V0:])
    norm = jnp.sum(z * z, axis=0, keepdims=True) * (-0.5 * LOG2E)
    parts = [a.astype(F32) for a in split3(norm)]
    sub = iota((T0 - V0, rows), 0)
    extra = jnp.where(jnp.logical_and(sub >= N0 - T0, sub < ONE - T0), 1.0, 0.0)
    for k in range(3):
        extra = jnp.where(sub == ONE - T0 + k, parts[k], extra)
    z = jnp.concatenate(
        split3(z * LOG2E) + (jnp.zeros((T0 - V0, rows), BF16), extra.astype(BF16)), axis=0
    )
    eight = task_ref[i]
    task = jnp.concatenate([eight[m : m + 1] for m in range(8)], axis=1)
    weight = look_up(tab, task.astype(jnp.int32))
    width = st.shape[0] // 5
    total = None
    for j in range(zc.shape[0] // tile):
        span = slice(j * tile, (j + 1) * tile)
        x = jnp.dot(zc[span, :], z, preferred_element_type=F32)
        kern = jnp.minimum(jnp.exp2(x).astype(BF16), jnp.asarray(1.0, BF16))
        kern_ref[span, :] = kern
        part = jnp.dot(st[: 4 * width, span], kern, preferred_element_type=F32)
        total = part if total is None else total + part
    low = weight[0:1] * total[:width]
    for q in range(1, 4):
        low = low + weight[q : q + 1] * total[q * width : (q + 1) * width]
    size = zc.shape[0] // 32
    count = rows // 2
    quarter = count // 4
    for k in range(2):
        lanes = slice(k * count, (k + 1) * count)
        start = pl.multiple_of(jnp.clip(4 * (2 * i + k) - 1, 0, 26) * size, size)
        band = pl.ds(start, 6 * size)
        same = zc[band, 128 + T0 : 129 + T0] == task[:, lanes].astype(BF16)
        kept = jnp.where(same, kern_ref[band, lanes], jnp.asarray(0.0, BF16))
        diag = jnp.dot(st[4 * width :, band], kept, preferred_element_type=F32)
        summed = low[:, lanes] + weight[4:5, lanes] * diag
        folded = jnp.concatenate(
            [summed[:, m * quarter : (m + 1) * quarter] for m in range(4)], axis=0
        ).T.reshape(chunks, 16, 128)
        span = slice(k * 16, k * 16 + 16)
        if last:
            folded = folded + before[:, span, :]
            mine[...] = folded
            own[span, :] = mine[own_chunk[0]]
        out[:, span, :] = folded.astype(out.dtype)


def product_call(own_chunk, table, gathered, cols, before=()):
    chunks, packed, _ = gathered.shape
    total = sum(c.size // 128 for c in cols)
    quarter = (packed - 16) // 2
    steps = quarter // 32
    rows = chunks * 128
    block = pl.BlockSpec((chunks, 32, 128), lambda i: (0, i, 0))
    out_specs, scratch = [block], []
    out_shape = [jax.ShapeDtypeStruct((chunks, quarter, 128), BF16 if before else F32)]
    if before:
        out_specs.append(pl.BlockSpec((32, 128), lambda i: (i, 0)))
        out_shape.append(jax.ShapeDtypeStruct((quarter, 128), F32))
        scratch.append(pltpu.VMEM((chunks, 16, 128), F32))
    return pl.pallas_call(
        functools.partial(product_kernel, 2048, len(cols), bool(before)),
        grid=(steps,),
        in_specs=[SMEM] + [VMEM] * (2 + len(cols)) + [block] * len(before),
        out_specs=out_specs,
        out_shape=out_shape,
        scratch_shapes=[
            pltpu.VMEM((total, rows), BF16),
            pltpu.VMEM((steps, 8, chunks * 16), F32),
            pltpu.VMEM((total, 256), BF16),
            pltpu.VMEM((5 * (T0 - V0), total), BF16),
        ]
        + scratch,
        compiler_params=LARGE,
        cost_estimate=pl.CostEstimate(
            flops=2 * steps * rows * total * 512, bytes_accessed=4 << 20, transcendentals=0
        ),
        name="product",
    )(own_chunk, table, gathered, *cols, *before)


def stack_kernel(count, *refs):
    if count == 0:
        refs[-1][...] = refs[0][...]
    for k in range(count):
        refs[-1][k] = refs[k][...]


def image_kernel(col, parts, own, vq, nv, pos, send):
    img = own[...] + nv[...]
    for k in range(parts.shape[0]):
        img = img + jnp.where(k == col[0], 0.0, parts[k].astype(F32))
    v = vq[...]

    def over(x):
        s = jnp.sum(x, axis=0, keepdims=True)
        return s[:, 0:32] + s[:, 32:64] + s[:, 64:96] + s[:, 96:128]

    vv, vi = over(v * v), over(v * img)
    ratio = jnp.where(vv > 0.0, vi / jnp.where(vv > 0.0, vv, 1.0), 0.0)
    rest = img - jnp.concatenate([ratio] * 4, axis=1) * v
    row = jnp.concatenate([vv, vi, over(rest * rest), jnp.zeros_like(vv)], axis=1)
    send[:, 0, :128] = img
    send[:, 0, 128:256] = v
    send[:, 0, 256:] = pos[...] + row


def final_kernel(got, residual, direction, alpha_out, beta_out):
    n = got.shape[0]
    rows = residual.shape[1]
    every = got[:, 0, 256:]
    turned = every.T

    def over(axis, pick):
        vv, vi, rr = (pick(k) for k in range(3))
        total_v = jnp.sum(vv, axis=axis, keepdims=True)
        total_i = jnp.sum(vi, axis=axis, keepdims=True)
        ratio = jnp.where(vv > 0.0, vi / jnp.where(vv > 0.0, vv, 1.0), 0.0)
        shift = ratio - total_i / total_v
        total_r = jnp.sum(rr + vv * (shift * shift), axis=axis, keepdims=True)
        alpha = total_v / total_i
        return alpha, alpha * alpha * total_r / total_v

    alpha, beta = over(1, lambda k: turned[32 * k : 32 * k + 32])
    sums = jnp.concatenate([alpha, beta, jnp.zeros((32, 126), F32)], axis=1).T
    alpha_out[...] = sums[0:1]
    beta_out[...] = sums[1:2]
    v = got[:, 0, 128:256].T
    res = v - jnp.concatenate([alpha] * 4, axis=0) * got[:, 0, :128].T
    pieces = split3(res) + (v.astype(BF16),)
    total = None
    for m in range(4):
        lanes = slice(m * 32, (m + 1) * 32)
        values = jnp.concatenate([p[lanes] for p in pieces], axis=0)
        place = every[:, 96 + m : 97 + m].astype(jnp.int32)
        onehot = (iota((n, rows), 1) == place).astype(BF16)
        part = jnp.dot(values, onehot, preferred_element_type=F32)
        total = part if total is None else total + part
    res_t = total[0:32] + total[32:64] + total[64:96]
    residual[...] = res_t
    direction[...] = res_t + beta * total[96:128]


def body(
    features,
    task_id,
    task_count,
    task_rank,
    probes,
    net_w,
    net_b,
    inv_scale,
    task_mix,
    task_diag,
    task_noise,
):
    rows = features.shape[0]
    n_row, n_col = lax.axis_size("row"), lax.axis_size("col")
    devices = n_row * n_col
    axes = ("row", "col")
    width = probes.shape[1]
    quarter = rows // 4
    col = lax.axis_index("col")
    own_chunk = (col // 4 * 2 + col % 2).astype(jnp.int32).reshape(1)
    groups = [[4 * x + z for x in range(n_col // 4) for z in pair] for pair in ((0, 1), (2, 3))]

    def over_rows(value):
        return lax.all_to_all(
            value, "col", split_axis=0, concat_axis=0, tiled=True, axis_index_groups=groups
        )

    def other_core(value):
        return lax.ppermute(value, "row", [(i, i ^ 1) for i in range(n_row)])

    shape = jax.ShapeDtypeStruct((quarter, 128), F32)
    cols, share, vq, nv, pos, table = pl.pallas_call(
        pack_kernel,
        in_specs=[VMEM] * 11,
        out_specs=[VMEM] * 6,
        out_shape=[
            jax.ShapeDtypeStruct((rows, 128), BF16),
            jax.ShapeDtypeStruct((n_col // 2, rows // 2 + 16, 128), BF16),
            shape,
            shape,
            shape,
            jax.ShapeDtypeStruct((8, task_count.shape[0]), F32),
        ],
        compiler_params=ALONE,
        name="pack",
    )(
        features.T,
        task_id.reshape(1, -1),
        task_count.reshape(1, -1),
        task_rank.reshape(1, -1),
        probes.T,
        net_w,
        net_b.reshape(1, -1),
        inv_scale.reshape(1, -1),
        task_mix.T,
        task_diag.reshape(1, -1),
        task_noise.reshape(1, -1),
    )
    gathered = over_rows(share)
    own_y = [cols] + [
        lax.ppermute(cols, "row", [(i, (i + 2 * k) % n_row) for i in range(n_row)])
        for k in range(1, n_row // 2)
    ]
    other_y = [other_core(c) for c in own_y]
    stacked = jax.ShapeDtypeStruct((len(own_y),) + cols.shape, BF16)
    anywhere = pl.BlockSpec(memory_space=pl.ANY)
    pair_y = pl.pallas_call(
        functools.partial(stack_kernel, len(own_y)),
        in_specs=[VMEM] * len(own_y) + [anywhere] * len(other_y),
        out_specs=VMEM,
        out_shape=stacked,
        compiler_params=PARAMS,
        name="stack",
    )(*own_y, *other_y)
    pair_y = lax.ppermute(pair_y, "col", [(i, i ^ 3) for i in range(n_col)])
    (sums,) = product_call(own_chunk, table, gathered, own_y + other_y)
    pair_y = pl.pallas_call(
        functools.partial(stack_kernel, 0),
        in_specs=[VMEM, anywhere],
        out_specs=VMEM,
        out_shape=stacked,
        compiler_params=PARAMS,
        name="gate",
    )(pair_y, sums)
    parts, own = product_call(own_chunk, table, gathered, [pair_y, other_core(pair_y)], (sums,))
    summed = over_rows(parts)
    send = pl.pallas_call(
        image_kernel,
        in_specs=[SMEM] + [VMEM] * 5,
        out_specs=VMEM,
        out_shape=jax.ShapeDtypeStruct((devices, 1, 384), F32),
        compiler_params=PARAMS,
        name="image",
    )(own_chunk, summed, own, vq, nv, pos)
    got = lax.all_to_all(send, ("row", "col"), split_axis=0, concat_axis=0, tiled=True)
    residual, direction, alpha, beta = pl.pallas_call(
        final_kernel,
        in_specs=[VMEM],
        out_specs=[VMEM] * 4,
        out_shape=[
            jax.ShapeDtypeStruct((width, rows), F32),
            jax.ShapeDtypeStruct((width, rows), F32),
            jax.ShapeDtypeStruct((1, width), F32),
            jax.ShapeDtypeStruct((1, width), F32),
        ],
        compiler_params=PARAMS,
        name="final",
    )(got)
    return residual.T, direction.T, alpha.reshape(width), beta.reshape(width)


def solution(mesh):
    axes = ("row", "col")
    return jax.shard_map(
        body,
        mesh=mesh,
        in_specs=(
            P(axes, None),
            P(axes),
            P(),
            P(axes),
            P(axes, None),
            P(),
            P(),
            P(),
            P(),
            P(),
            P(),
        ),
        out_specs=(P(axes, None), P(axes, None), P(), P()),
        check_vma=False,
    )
```

```python
import functools
import math

import jax
import jax.numpy as jnp
from jax import lax
from jax.experimental import pallas as pl
from jax.experimental.pallas import tpu as pltpu
from jax.sharding import PartitionSpec as P

F32 = jnp.float32
BF16 = jnp.bfloat16
VMEM = pl.BlockSpec(memory_space=pltpu.VMEM)
SMEM = pl.BlockSpec(memory_space=pltpu.SMEM)
PARAMS = pltpu.CompilerParams(vmem_limit_bytes=16 * 1024 * 1024)
ALONE = pltpu.CompilerParams(vmem_limit_bytes=60 * 1024 * 1024)
LARGE = pltpu.CompilerParams(vmem_limit_bytes=36 * 1024 * 1024)
V0, T0, N0, ONE, P0, S0, W0 = 64, 96, 97, 100, 103, 105, 112
LOG2E = math.log2(math.e)


def iota(shape, dim):
    return lax.broadcasted_iota(jnp.int32, shape, dim)


def split3(x):
    hi = x.astype(BF16)
    rest = x - hi.astype(F32)
    mid = rest.astype(BF16)
    low = (rest - mid.astype(F32)).astype(BF16)
    return hi, mid, low


def look_up(table, task):
    hit = (iota((table.shape[1], task.shape[1]), 0) == task).astype(BF16)
    tab = jnp.concatenate(split3(table), axis=0)
    got = jnp.dot(tab, hit, preferred_element_type=F32)
    return got[0:8] + got[8:16] + got[16:24]


def order_of(tid, cnt, rank):
    rows, ntask = tid.shape[1], cnt.shape[1]
    counts = cnt[...].astype(F32)
    before = iota((ntask, ntask), 1) < iota((ntask, ntask), 0)
    start = jnp.sum(jnp.where(before, counts, 0.0), axis=1, keepdims=True)
    hit = iota((ntask, rows), 0) == tid[...]
    pos = jnp.sum(jnp.where(hit, start, 0.0), axis=0, keepdims=True) + rank[...].astype(F32)
    pos_col = jnp.concatenate([pos, jnp.zeros((7, rows), F32)], axis=0).T[:, 0:1]
    return pos, jnp.sum((pos_col < pos).astype(F32), axis=0, keepdims=True)


def pack_kernel(
    feat, tid, cnt, rank, probes, net_w, net_b, scale, mix, diag, noise_in,
    cols, rows_out, vq_out, nv_out, pos_out, table_out,
):
    rows = feat.shape[1]
    width = probes.shape[0]
    pos, order = order_of(tid, cnt, rank)
    task = tid[...]
    table = jnp.concatenate(
        [mix[...], diag[...], noise_in[...], jnp.zeros((2, mix.shape[1]), F32)], axis=0
    )
    table_out[...] = table
    column = jnp.concatenate([net_b[...], scale[...], jnp.zeros((6, 64), F32)], axis=0).T
    hidden = jnp.tanh(
        lax.dot_general(
            net_w[...], feat[...], (((0,), (0,)), ((), ())), preferred_element_type=F32
        )
        + column[:, 0:1]
    )
    latent = (hidden * column[:, 1:2]).astype(BF16)
    lat = latent.astype(F32)
    norm = jnp.sum(lat * lat, axis=0, keepdims=True) * (-0.5 * LOG2E)
    local = pos - jnp.floor(pos * (1.0 / rows)) * rows
    high = jnp.floor(local * (1.0 / 16.0))
    found = look_up(table, task)
    extra = jnp.concatenate(
        [task.astype(F32)]
        + [a.astype(F32) for a in split3(norm)]
        + [jnp.ones((3, rows), F32), high, local - 16.0 * high]
        + [a.astype(F32) for a in split3(found[5:6])]
        + [jnp.zeros((4, rows), F32)]
        + [a.astype(F32) for a in split3(found[0:4])]
        + [jnp.zeros((4, rows), F32)],
        axis=0,
    ).astype(BF16)
    whole = jnp.concatenate([latent, probes[...], extra], axis=0)
    tile = jnp.floor(order * (1.0 / 64.0))
    inner = order - tile * 64.0
    block = jnp.floor(inner * 0.25)
    order_r = tile * 64.0 + (inner - block * 4.0) * 16.0 + block
    square = iota((rows, rows), 0)
    place_c = (square == order.astype(jnp.int32)).astype(BF16)
    place_r = (square == order_r.astype(jnp.int32)).astype(BF16)
    turn = (((1,), (1,)), ((), ()))
    data = lax.dot_general(place_c, whole, turn, preferred_element_type=F32).astype(BF16)
    cols[...] = data
    data = lax.dot_general(place_r, whole, turn, preferred_element_type=F32)
    half = rows // 2
    pair = jnp.concatenate([data[:half, :V0], data[half:, :V0]], axis=1).astype(BF16)
    at = (iota((16, rows), 1) % 16 == iota((16, rows), 0)).astype(BF16)
    group = jnp.where(iota((rows, 128), 0) // 16 == iota((rows, 128), 1), data[:, T0 : T0 + 1], 0.0)
    tasks = jnp.dot(at, group.astype(BF16), preferred_element_type=F32).astype(BF16)
    for k in range(rows_out.shape[0]):
        rows_out[k, :half, :] = pair
        rows_out[k, half:, :] = tasks
    place = data[:, P0 : P0 + 1] * 16.0 + data[:, P0 + 1 : P0 + 2]
    noise_c = data[:, S0 : S0 + 1] + data[:, S0 + 1 : S0 + 2] + data[:, S0 + 2 : S0 + 3]
    v = data[:, V0:T0]
    nv = noise_c * v

    def fold(x, m):
        return jnp.concatenate(
            [x[t * 64 + m * 16 : t * 64 + m * 16 + 16] for t in range(rows // 64)], axis=0
        )

    vq_out[...] = jnp.concatenate([fold(v, m) for m in range(4)], axis=1)
    nv_out[...] = jnp.concatenate([fold(nv, m) for m in range(4)], axis=1)
    lane = iota((rows // 4, 128), 1)
    posq = jnp.zeros((rows // 4, 128), F32)
    for m in range(4):
        posq = jnp.where(lane == 3 * width + m, fold(place, m), posq)
    pos_out[...] = posq


def prepare_cols(cols, zc, st):
    chunks = []
    for c in cols:
        chunks += [c] if len(c.shape) == 2 else [c.at[h] for h in range(c.shape[0])]
    rows = chunks[0].shape[0]
    size = 4 * 16 * len(chunks)
    width = T0 - V0
    for k in range(rows // 64):
        data = jnp.concatenate(
            [c[g * 16 : g * 16 + 16, :] for g in range(4 * k, 4 * k + 4) for c in chunks],
            axis=0,
        )
        span = slice(k * size, (k + 1) * size)
        wide = data.astype(F32)
        zc[span, 128:] = data
        zc[span, :128] = jnp.where(iota((size, 128), 1) < V0, wide, pltpu.roll(wide, V0, 1)).astype(BF16)
        turned = wide.T
        weight = turned[W0 : W0 + 4] + turned[W0 + 4 : W0 + 8] + turned[W0 + 8 : W0 + 12]
        values = turned[V0:T0]
        for q in range(4):
            st[q * width : (q + 1) * width, span] = (weight[q : q + 1] * values).astype(BF16)
        st[4 * width :, span] = values.astype(BF16)


def product_kernel(tile, pieces, last, own_chunk, table, gathered, *refs):
    cols, refs = refs[:pieces], refs[pieces:]
    if last:
        before, out, own, kern_ref, task_ref, zc, st, mine = refs
    else:
        out, kern_ref, task_ref, zc, st = refs
    i = pl.program_id(0)
    steps = pl.num_programs(0)
    chunks = gathered.shape[0]
    half = gathered.shape[1] - 16
    tab = table[...]

    @pl.when(i == 0)
    def _():
        every = gathered[:, half:, :].reshape(chunks * 16, 128).astype(F32).T
        for k in range(task_ref.shape[0]):
            task_ref[k] = every[8 * k : 8 * k + 8]
        prepare_cols(cols, zc, st)

    first = pl.multiple_of(lax.rem(i, steps // 2) * 128, 128)
    blocks = [gathered[k, pl.ds(first, 128), :] for k in range(chunks)]
    data = jnp.concatenate(
        [b[g * 16 : g * 16 + 16, :] for g in range(8) for b in blocks], axis=0
    )
    rows = data.shape[0]
    turned = data.astype(F32).T
    z = jnp.where(i < steps // 2, turned[:V0], turned[V0:])
    norm = jnp.sum(z * z, axis=0, keepdims=True) * (-0.5 * LOG2E)
    parts = [a.astype(F32) for a in split3(norm)]
    sub = iota((T0 - V0, rows), 0)
    extra = jnp.where(jnp.logical_and(sub >= N0 - T0, sub < ONE - T0), 1.0, 0.0)
    for k in range(3):
        extra = jnp.where(sub == ONE - T0 + k, parts[k], extra)
    z = jnp.concatenate(
        split3(z * LOG2E) + (jnp.zeros((T0 - V0, rows), BF16), extra.astype(BF16)), axis=0
    )
    eight = task_ref[i]
    task = jnp.concatenate([eight[m : m + 1] for m in range(8)], axis=1)
    weight = look_up(tab, task.astype(jnp.int32))
    width = st.shape[0] // 5
    total = None
    for j in range(zc.shape[0] // tile):
        span = slice(j * tile, (j + 1) * tile)
        x = jnp.dot(zc[span, :], z, preferred_element_type=F32)
        kern = jnp.minimum(jnp.exp2(x).astype(BF16), jnp.asarray(1.0, BF16))
        kern_ref[span, :] = kern
        part = jnp.dot(st[: 4 * width, span], kern, preferred_element_type=F32)
        total = part if total is None else total + part
    low = weight[0:1] * total[:width]
    for q in range(1, 4):
        low = low + weight[q : q + 1] * total[q * width : (q + 1) * width]
    size = zc.shape[0] // 32
    count = rows // 2
    quarter = count // 4
    for k in range(2):
        lanes = slice(k * count, (k + 1) * count)
        start = pl.multiple_of(jnp.clip(4 * (2 * i + k) - 1, 0, 26) * size, size)
        band = pl.ds(start, 6 * size)
        same = zc[band, 128 + T0 : 129 + T0] == task[:, lanes].astype(BF16)
        kept = jnp.where(same, kern_ref[band, lanes], jnp.asarray(0.0, BF16))
        diag = jnp.dot(st[4 * width :, band], kept, preferred_element_type=F32)
        summed = low[:, lanes] + weight[4:5, lanes] * diag
        folded = jnp.concatenate(
            [summed[:, m * quarter : (m + 1) * quarter] for m in range(4)], axis=0
        ).T.reshape(chunks, 16, 128)
        span = slice(k * 16, k * 16 + 16)
        if last:
            folded = folded + before[:, span, :]
            mine[...] = folded
            own[span, :] = mine[own_chunk[0]]
        out[:, span, :] = folded.astype(out.dtype)


def product_call(own_chunk, table, gathered, cols, before=()):
    chunks, packed, _ = gathered.shape
    total = sum(c.size // 128 for c in cols)
    quarter = (packed - 16) // 2
    steps = quarter // 32
    rows = chunks * 128
    block = pl.BlockSpec((chunks, 32, 128), lambda i: (0, i, 0))
    out_specs, scratch = [block], []
    out_shape = [jax.ShapeDtypeStruct((chunks, quarter, 128), BF16 if before else F32)]
    if before:
        out_specs.append(pl.BlockSpec((32, 128), lambda i: (i, 0)))
        out_shape.append(jax.ShapeDtypeStruct((quarter, 128), F32))
        scratch.append(pltpu.VMEM((chunks, 16, 128), F32))
    return pl.pallas_call(
        functools.partial(product_kernel, 2048, len(cols), bool(before)),
        grid=(steps,),
        in_specs=[SMEM] + [VMEM] * (2 + len(cols)) + [block] * len(before),
        out_specs=out_specs,
        out_shape=out_shape,
        scratch_shapes=[
            pltpu.VMEM((total, rows), BF16),
            pltpu.VMEM((steps, 8, chunks * 16), F32),
            pltpu.VMEM((total, 256), BF16),
            pltpu.VMEM((5 * (T0 - V0), total), BF16),
        ]
        + scratch,
        compiler_params=LARGE,
        cost_estimate=pl.CostEstimate(
            flops=2 * steps * rows * total * 512, bytes_accessed=4 << 20, transcendentals=0
        ),
        name="product",
    )(own_chunk, table, gathered, *cols, *before)


def stack_kernel(count, *refs):
    if count == 0:
        refs[-1][...] = refs[0][...]
    for k in range(count):
        refs[-1][k] = refs[k][...]


def image_kernel(col, parts, own, vq, nv, pos, send):
    img = own[...] + nv[...]
    for k in range(parts.shape[0]):
        img = img + jnp.where(k == col[0], 0.0, parts[k].astype(F32))
    v = vq[...]

    def over(x):
        s = jnp.sum(x, axis=0, keepdims=True)
        return s[:, 0:32] + s[:, 32:64] + s[:, 64:96] + s[:, 96:128]

    vv, vi = over(v * v), over(v * img)
    ratio = jnp.where(vv > 0.0, vi / jnp.where(vv > 0.0, vv, 1.0), 0.0)
    rest = img - jnp.concatenate([ratio] * 4, axis=1) * v
    row = jnp.concatenate([vv, vi, over(rest * rest), jnp.zeros_like(vv)], axis=1)
    send[:, 0, :128] = img
    send[:, 0, 128:256] = v
    send[:, 0, 256:] = pos[...] + row


def final_kernel(got, residual, direction, alpha_out, beta_out):
    n = got.shape[0]
    rows = residual.shape[1]
    every = got[:, 0, 256:]
    turned = every.T

    def over(axis, pick):
        vv, vi, rr = (pick(k) for k in range(3))
        total_v = jnp.sum(vv, axis=axis, keepdims=True)
        total_i = jnp.sum(vi, axis=axis, keepdims=True)
        ratio = jnp.where(vv > 0.0, vi / jnp.where(vv > 0.0, vv, 1.0), 0.0)
        shift = ratio - total_i / total_v
        total_r = jnp.sum(rr + vv * (shift * shift), axis=axis, keepdims=True)
        alpha = total_v / total_i
        return alpha, alpha * alpha * total_r / total_v

    alpha, beta = over(1, lambda k: turned[32 * k : 32 * k + 32])
    sums = jnp.concatenate([alpha, beta, jnp.zeros((32, 126), F32)], axis=1).T
    alpha_out[...] = sums[0:1]
    beta_out[...] = sums[1:2]
    v = got[:, 0, 128:256].T
    res = v - jnp.concatenate([alpha] * 4, axis=0) * got[:, 0, :128].T
    pieces = split3(res) + (v.astype(BF16),)
    total = None
    for m in range(4):
        lanes = slice(m * 32, (m + 1) * 32)
        values = jnp.concatenate([p[lanes] for p in pieces], axis=0)
        place = every[:, 96 + m : 97 + m].astype(jnp.int32)
        onehot = (iota((n, rows), 1) == place).astype(BF16)
        part = jnp.dot(values, onehot, preferred_element_type=F32)
        total = part if total is None else total + part
    res_t = total[0:32] + total[32:64] + total[64:96]
    residual[...] = res_t
    direction[...] = res_t + beta * total[96:128]


def body(
    features,
    task_id,
    task_count,
    task_rank,
    probes,
    net_w,
    net_b,
    inv_scale,
    task_mix,
    task_diag,
    task_noise,
):
    rows = features.shape[0]
    n_row, n_col = lax.axis_size("row"), lax.axis_size("col")
    devices = n_row * n_col
    axes = ("row", "col")
    width = probes.shape[1]
    quarter = rows // 4
    col = lax.axis_index("col")
    own_chunk = (col // 4 * 2 + col % 2).astype(jnp.int32).reshape(1)
    groups = [[4 * x + z for x in range(n_col // 4) for z in pair] for pair in ((0, 1), (2, 3))]

    def over_rows(value):
        return lax.all_to_all(
            value, "col", split_axis=0, concat_axis=0, tiled=True, axis_index_groups=groups
        )

    def other_core(value):
        return lax.ppermute(value, "row", [(i, i ^ 1) for i in range(n_row)])

    shape = jax.ShapeDtypeStruct((quarter, 128), F32)
    cols, share, vq, nv, pos, table = pl.pallas_call(
        pack_kernel,
        in_specs=[VMEM] * 11,
        out_specs=[VMEM] * 6,
        out_shape=[
            jax.ShapeDtypeStruct((rows, 128), BF16),
            jax.ShapeDtypeStruct((n_col // 2, rows // 2 + 16, 128), BF16),
            shape,
            shape,
            shape,
            jax.ShapeDtypeStruct((8, task_count.shape[0]), F32),
        ],
        compiler_params=ALONE,
        name="pack",
    )(
        features.T,
        task_id.reshape(1, -1),
        task_count.reshape(1, -1),
        task_rank.reshape(1, -1),
        probes.T,
        net_w,
        net_b.reshape(1, -1),
        inv_scale.reshape(1, -1),
        task_mix.T,
        task_diag.reshape(1, -1),
        task_noise.reshape(1, -1),
    )
    gathered = over_rows(share)
    own_y = [cols] + [
        lax.ppermute(cols, "row", [(i, (i + 2 * k) % n_row) for i in range(n_row)])
        for k in range(1, n_row // 2)
    ]
    other_y = [other_core(c) for c in own_y]
    stacked = jax.ShapeDtypeStruct((len(own_y),) + cols.shape, BF16)
    anywhere = pl.BlockSpec(memory_space=pl.ANY)
    pair_y = pl.pallas_call(
        functools.partial(stack_kernel, len(own_y)),
        in_specs=[VMEM] * len(own_y),
        out_specs=VMEM,
        out_shape=stacked,
        compiler_params=PARAMS,
        name="stack",
    )(*own_y)
    pair_y = lax.ppermute(pair_y, "col", [(i, i ^ 3) for i in range(n_col)])
    (sums,) = product_call(own_chunk, table, gathered, own_y + other_y)
    pair_y = pl.pallas_call(
        functools.partial(stack_kernel, 0),
        in_specs=[VMEM, anywhere],
        out_specs=VMEM,
        out_shape=stacked,
        compiler_params=PARAMS,
        name="gate",
    )(pair_y, sums)
    parts, own = product_call(own_chunk, table, gathered, [pair_y, other_core(pair_y)], (sums,))
    summed = over_rows(parts)
    send = pl.pallas_call(
        image_kernel,
        in_specs=[SMEM] + [VMEM] * 5,
        out_specs=VMEM,
        out_shape=jax.ShapeDtypeStruct((devices, 1, 384), F32),
        compiler_params=PARAMS,
        name="image",
    )(own_chunk, summed, own, vq, nv, pos)
    got = lax.all_to_all(send, ("row", "col"), split_axis=0, concat_axis=0, tiled=True)
    residual, direction, alpha, beta = pl.pallas_call(
        final_kernel,
        in_specs=[VMEM],
        out_specs=[VMEM] * 4,
        out_shape=[
            jax.ShapeDtypeStruct((width, rows), F32),
            jax.ShapeDtypeStruct((width, rows), F32),
            jax.ShapeDtypeStruct((1, width), F32),
            jax.ShapeDtypeStruct((1, width), F32),
        ],
        compiler_params=PARAMS,
        name="final",
    )(got)
    return residual.T, direction.T, alpha.reshape(width), beta.reshape(width)


def solution(mesh):
    axes = ("row", "col")
    return jax.shard_map(
        body,
        mesh=mesh,
        in_specs=(
            P(axes, None),
            P(axes),
            P(),
            P(axes),
            P(axes, None),
            P(),
            P(),
            P(),
            P(),
            P(),
            P(),
        ),
        out_specs=(P(axes, None), P(axes, None), P(), P()),
        check_vma=False,
    )
```

```python
import functools
import math

import jax
import jax.numpy as jnp
from jax import lax
from jax.experimental import pallas as pl
from jax.experimental.pallas import tpu as pltpu
from jax.sharding import PartitionSpec as P

F32 = jnp.float32
BF16 = jnp.bfloat16
VMEM = pl.BlockSpec(memory_space=pltpu.VMEM)
SMEM = pl.BlockSpec(memory_space=pltpu.SMEM)
PARAMS = pltpu.CompilerParams(vmem_limit_bytes=16 * 1024 * 1024)
ALONE = pltpu.CompilerParams(vmem_limit_bytes=60 * 1024 * 1024)
LARGE = pltpu.CompilerParams(vmem_limit_bytes=36 * 1024 * 1024)
V0, T0, N0, ONE, P0, S0, W0 = 64, 96, 97, 100, 103, 105, 112
LOG2E = math.log2(math.e)


def iota(shape, dim):
    return lax.broadcasted_iota(jnp.int32, shape, dim)


def split3(x):
    hi = x.astype(BF16)
    rest = x - hi.astype(F32)
    mid = rest.astype(BF16)
    low = (rest - mid.astype(F32)).astype(BF16)
    return hi, mid, low


def look_up(table, task):
    hit = (iota((table.shape[1], task.shape[1]), 0) == task).astype(BF16)
    tab = jnp.concatenate(split3(table), axis=0)
    got = jnp.dot(tab, hit, preferred_element_type=F32)
    return got[0:8] + got[8:16] + got[16:24]


def order_of(tid, cnt, rank):
    rows, ntask = tid.shape[1], cnt.shape[1]
    counts = cnt[...].astype(F32)
    before = iota((ntask, ntask), 1) < iota((ntask, ntask), 0)
    start = jnp.sum(jnp.where(before, counts, 0.0), axis=1, keepdims=True)
    hit = iota((ntask, rows), 0) == tid[...]
    pos = jnp.sum(jnp.where(hit, start, 0.0), axis=0, keepdims=True) + rank[...].astype(F32)
    pos_col = jnp.concatenate([pos, jnp.zeros((7, rows), F32)], axis=0).T[:, 0:1]
    return pos, jnp.sum((pos_col < pos).astype(F32), axis=0, keepdims=True)


def pack_kernel(
    feat, tid, cnt, rank, probes, net_w, net_b, scale, mix, diag, noise_in,
    cols, rows_out, vq_out, nv_out, pos_out, table_out,
):
    rows = feat.shape[1]
    width = probes.shape[0]
    pos, order = order_of(tid, cnt, rank)
    task = tid[...]
    table = jnp.concatenate(
        [mix[...], diag[...], noise_in[...], jnp.zeros((2, mix.shape[1]), F32)], axis=0
    )
    table_out[...] = table
    column = jnp.concatenate([net_b[...], scale[...], jnp.zeros((6, 64), F32)], axis=0).T
    hidden = jnp.tanh(
        lax.dot_general(
            net_w[...], feat[...], (((0,), (0,)), ((), ())), preferred_element_type=F32
        )
        + column[:, 0:1]
    )
    latent = (hidden * column[:, 1:2]).astype(BF16)
    lat = latent.astype(F32)
    norm = jnp.sum(lat * lat, axis=0, keepdims=True) * (-0.5 * LOG2E)
    local = pos - jnp.floor(pos * (1.0 / rows)) * rows
    high = jnp.floor(local * (1.0 / 16.0))
    found = look_up(table, task)
    extra = jnp.concatenate(
        [task.astype(F32)]
        + [a.astype(F32) for a in split3(norm)]
        + [jnp.ones((3, rows), F32), high, local - 16.0 * high]
        + [a.astype(F32) for a in split3(found[5:6])]
        + [jnp.zeros((4, rows), F32)]
        + [a.astype(F32) for a in split3(found[0:4])]
        + [jnp.zeros((4, rows), F32)],
        axis=0,
    ).astype(BF16)
    whole = jnp.concatenate([latent, probes[...], extra], axis=0)
    tile = jnp.floor(order * (1.0 / 64.0))
    inner = order - tile * 64.0
    block = jnp.floor(inner * 0.25)
    order_r = tile * 64.0 + (inner - block * 4.0) * 16.0 + block
    square = iota((rows, rows), 0)
    place_c = (square == order.astype(jnp.int32)).astype(BF16)
    place_r = (square == order_r.astype(jnp.int32)).astype(BF16)
    turn = (((1,), (1,)), ((), ()))
    data = lax.dot_general(place_c, whole, turn, preferred_element_type=F32).astype(BF16)
    cols[...] = data
    data = lax.dot_general(place_r, whole, turn, preferred_element_type=F32)
    half = rows // 2
    pair = jnp.concatenate([data[:half, :V0], data[half:, :V0]], axis=1).astype(BF16)
    at = (iota((16, rows), 1) % 16 == iota((16, rows), 0)).astype(BF16)
    group = jnp.where(iota((rows, 128), 0) // 16 == iota((rows, 128), 1), data[:, T0 : T0 + 1], 0.0)
    tasks = jnp.dot(at, group.astype(BF16), preferred_element_type=F32).astype(BF16)
    for k in range(rows_out.shape[0]):
        rows_out[k, :half, :] = pair
        rows_out[k, half:, :] = tasks
    place = data[:, P0 : P0 + 1] * 16.0 + data[:, P0 + 1 : P0 + 2]
    noise_c = data[:, S0 : S0 + 1] + data[:, S0 + 1 : S0 + 2] + data[:, S0 + 2 : S0 + 3]
    v = data[:, V0:T0]
    nv = noise_c * v

    def fold(x, m):
        return jnp.concatenate(
            [x[t * 64 + m * 16 : t * 64 + m * 16 + 16] for t in range(rows // 64)], axis=0
        )

    vq_out[...] = jnp.concatenate([fold(v, m) for m in range(4)], axis=1)
    nv_out[...] = jnp.concatenate([fold(nv, m) for m in range(4)], axis=1)
    lane = iota((rows // 4, 128), 1)
    posq = jnp.zeros((rows // 4, 128), F32)
    for m in range(4):
        posq = jnp.where(lane == 3 * width + m, fold(place, m), posq)
    pos_out[...] = posq


def prepare_cols(cols, zc, st):
    chunks = []
    for c in cols:
        chunks += [c] if len(c.shape) == 2 else [c.at[h] for h in range(c.shape[0])]
    rows = chunks[0].shape[0]
    size = 4 * 16 * len(chunks)
    width = T0 - V0
    for k in range(rows // 64):
        data = jnp.concatenate(
            [c[g * 16 : g * 16 + 16, :] for g in range(4 * k, 4 * k + 4) for c in chunks],
            axis=0,
        )
        span = slice(k * size, (k + 1) * size)
        wide = data.astype(F32)
        zc[span, 128:] = data
        zc[span, :128] = jnp.where(iota((size, 128), 1) < V0, wide, pltpu.roll(wide, V0, 1)).astype(BF16)
        turned = wide.T
        weight = turned[W0 : W0 + 4] + turned[W0 + 4 : W0 + 8] + turned[W0 + 8 : W0 + 12]
        values = turned[V0:T0]
        for q in range(4):
            st[q * width : (q + 1) * width, span] = (weight[q : q + 1] * values).astype(BF16)
        st[4 * width :, span] = values.astype(BF16)


def product_kernel(tile, pieces, last, own_chunk, table, gathered, *refs):
    cols, refs = refs[:pieces], refs[pieces:]
    if last:
        before, out, own, kern_ref, task_ref, zc, st, mine = refs
    else:
        out, kern_ref, task_ref, zc, st = refs
    i = pl.program_id(0)
    steps = pl.num_programs(0)
    chunks = gathered.shape[0]
    half = gathered.shape[1] - 16
    tab = table[...]

    @pl.when(i == 0)
    def _():
        every = gathered[:, half:, :].reshape(chunks * 16, 128).astype(F32).T
        for k in range(task_ref.shape[0]):
            task_ref[k] = every[8 * k : 8 * k + 8]
        prepare_cols(cols, zc, st)

    first = pl.multiple_of(lax.rem(i, steps // 2) * 128, 128)
    blocks = [gathered[k, pl.ds(first, 128), :] for k in range(chunks)]
    data = jnp.concatenate(
        [b[g * 16 : g * 16 + 16, :] for g in range(8) for b in blocks], axis=0
    )
    rows = data.shape[0]
    turned = data.astype(F32).T
    z = jnp.where(i < steps // 2, turned[:V0], turned[V0:])
    norm = jnp.sum(z * z, axis=0, keepdims=True) * (-0.5 * LOG2E)
    parts = [a.astype(F32) for a in split3(norm)]
    sub = iota((T0 - V0, rows), 0)
    extra = jnp.where(jnp.logical_and(sub >= N0 - T0, sub < ONE - T0), 1.0, 0.0)
    for k in range(3):
        extra = jnp.where(sub == ONE - T0 + k, parts[k], extra)
    z = jnp.concatenate(
        split3(z * LOG2E) + (jnp.zeros((T0 - V0, rows), BF16), extra.astype(BF16)), axis=0
    )
    eight = task_ref[i]
    task = jnp.concatenate([eight[m : m + 1] for m in range(8)], axis=1)
    weight = look_up(tab, task.astype(jnp.int32))
    width = st.shape[0] // 5
    total = None
    for j in range(zc.shape[0] // tile):
        span = slice(j * tile, (j + 1) * tile)
        x = jnp.dot(zc[span, :], z, preferred_element_type=F32)
        kern = jnp.minimum(jnp.exp2(x).astype(BF16), jnp.asarray(1.0, BF16))
        kern_ref[span, :] = kern
        part = jnp.dot(st[: 4 * width, span], kern, preferred_element_type=F32)
        total = part if total is None else total + part
    low = weight[0:1] * total[:width]
    for q in range(1, 4):
        low = low + weight[q : q + 1] * total[q * width : (q + 1) * width]
    size = zc.shape[0] // 32
    count = rows // 2
    quarter = count // 4
    for k in range(2):
        lanes = slice(k * count, (k + 1) * count)
        start = pl.multiple_of(jnp.clip(4 * (2 * i + k) - 1, 0, 26) * size, size)
        band = pl.ds(start, 6 * size)
        same = zc[band, 128 + T0 : 129 + T0] == task[:, lanes].astype(BF16)
        kept = jnp.where(same, kern_ref[band, lanes], jnp.asarray(0.0, BF16))
        diag = jnp.dot(st[4 * width :, band], kept, preferred_element_type=F32)
        summed = low[:, lanes] + weight[4:5, lanes] * diag
        folded = jnp.concatenate(
            [summed[:, m * quarter : (m + 1) * quarter] for m in range(4)], axis=0
        ).T.reshape(chunks, 16, 128)
        span = slice(k * 16, k * 16 + 16)
        if last:
            folded = folded + before[:, span, :]
            mine[...] = folded
            own[span, :] = mine[own_chunk[0]]
        out[:, span, :] = folded.astype(out.dtype)


def product_call(own_chunk, table, gathered, cols, before=()):
    chunks, packed, _ = gathered.shape
    total = sum(c.size // 128 for c in cols)
    quarter = (packed - 16) // 2
    steps = quarter // 32
    rows = chunks * 128
    block = pl.BlockSpec((chunks, 32, 128), lambda i: (0, i, 0))
    out_specs, scratch = [block], []
    out_shape = [jax.ShapeDtypeStruct((chunks, quarter, 128), BF16 if before else F32)]
    if before:
        out_specs.append(pl.BlockSpec((32, 128), lambda i: (i, 0)))
        out_shape.append(jax.ShapeDtypeStruct((quarter, 128), F32))
        scratch.append(pltpu.VMEM((chunks, 16, 128), F32))
    return pl.pallas_call(
        functools.partial(product_kernel, 2048, len(cols), bool(before)),
        grid=(steps,),
        in_specs=[SMEM] + [VMEM] * (2 + len(cols)) + [block] * len(before),
        out_specs=out_specs,
        out_shape=out_shape,
        scratch_shapes=[
            pltpu.VMEM((total, rows), BF16),
            pltpu.VMEM((steps, 8, chunks * 16), F32),
            pltpu.VMEM((total, 256), BF16),
            pltpu.VMEM((5 * (T0 - V0), total), BF16),
        ]
        + scratch,
        compiler_params=LARGE,
        cost_estimate=pl.CostEstimate(
            flops=2 * steps * rows * total * 512, bytes_accessed=4 << 20, transcendentals=0
        ),
        name="product",
    )(own_chunk, table, gathered, *cols, *before)


def stack_kernel(count, *refs):
    if count == 0:
        refs[-1][...] = refs[0][...]
    for k in range(count):
        refs[-1][k] = refs[k][...]


def image_kernel(col, parts, own, vq, nv, pos, send):
    img = own[...] + nv[...]
    for k in range(parts.shape[0]):
        img = img + jnp.where(k == col[0], 0.0, parts[k].astype(F32))
    v = vq[...]

    def over(x):
        s = jnp.sum(x, axis=0, keepdims=True)
        return s[:, 0:32] + s[:, 32:64] + s[:, 64:96] + s[:, 96:128]

    vv, vi = over(v * v), over(v * img)
    ratio = jnp.where(vv > 0.0, vi / jnp.where(vv > 0.0, vv, 1.0), 0.0)
    rest = img - jnp.concatenate([ratio] * 4, axis=1) * v
    row = jnp.concatenate([vv, vi, over(rest * rest), jnp.zeros_like(vv)], axis=1)
    send[:, 0, :128] = img
    send[:, 0, 128:256] = v
    send[:, 0, 256:] = pos[...] + row


def final_kernel(got, residual, direction, alpha_out, beta_out):
    n = got.shape[0]
    rows = residual.shape[1]
    every = got[:, 0, 256:]
    turned = every.T

    def over(axis, pick):
        vv, vi, rr = (pick(k) for k in range(3))
        total_v = jnp.sum(vv, axis=axis, keepdims=True)
        total_i = jnp.sum(vi, axis=axis, keepdims=True)
        ratio = jnp.where(vv > 0.0, vi / jnp.where(vv > 0.0, vv, 1.0), 0.0)
        shift = ratio - total_i / total_v
        total_r = jnp.sum(rr + vv * (shift * shift), axis=axis, keepdims=True)
        alpha = total_v / total_i
        return alpha, alpha * alpha * total_r / total_v

    alpha, beta = over(1, lambda k: turned[32 * k : 32 * k + 32])
    sums = jnp.concatenate([alpha, beta, jnp.zeros((32, 126), F32)], axis=1).T
    alpha_out[...] = sums[0:1]
    beta_out[...] = sums[1:2]
    v = got[:, 0, 128:256].T
    res = v - jnp.concatenate([alpha] * 4, axis=0) * got[:, 0, :128].T
    pieces = split3(res) + (v.astype(BF16),)
    total = None
    for m in range(4):
        lanes = slice(m * 32, (m + 1) * 32)
        values = jnp.concatenate([p[lanes] for p in pieces], axis=0)
        place = every[:, 96 + m : 97 + m].astype(jnp.int32)
        onehot = (iota((n, rows), 1) == place).astype(BF16)
        part = jnp.dot(values, onehot, preferred_element_type=F32)
        total = part if total is None else total + part
    res_t = total[0:32] + total[32:64] + total[64:96]
    residual[...] = res_t
    direction[...] = res_t + beta * total[96:128]


def body(
    features,
    task_id,
    task_count,
    task_rank,
    probes,
    net_w,
    net_b,
    inv_scale,
    task_mix,
    task_diag,
    task_noise,
):
    rows = features.shape[0]
    n_row, n_col = lax.axis_size("row"), lax.axis_size("col")
    devices = n_row * n_col
    axes = ("row", "col")
    width = probes.shape[1]
    quarter = rows // 4
    col = lax.axis_index("col")
    own_chunk = (col // 4 * 2 + col % 2).astype(jnp.int32).reshape(1)
    groups = [[4 * x + z for x in range(n_col // 4) for z in pair] for pair in ((0, 1), (2, 3))]

    def over_rows(value):
        return lax.all_to_all(
            value, "col", split_axis=0, concat_axis=0, tiled=True, axis_index_groups=groups
        )

    def other_core(value):
        return lax.ppermute(value, "row", [(i, i ^ 1) for i in range(n_row)])

    shape = jax.ShapeDtypeStruct((quarter, 128), F32)
    cols, share, vq, nv, pos, table = pl.pallas_call(
        pack_kernel,
        in_specs=[VMEM] * 11,
        out_specs=[VMEM] * 6,
        out_shape=[
            jax.ShapeDtypeStruct((rows, 128), BF16),
            jax.ShapeDtypeStruct((n_col // 2, rows // 2 + 16, 128), BF16),
            shape,
            shape,
            shape,
            jax.ShapeDtypeStruct((8, task_count.shape[0]), F32),
        ],
        compiler_params=ALONE,
        name="pack",
    )(
        features.T,
        task_id.reshape(1, -1),
        task_count.reshape(1, -1),
        task_rank.reshape(1, -1),
        probes.T,
        net_w,
        net_b.reshape(1, -1),
        inv_scale.reshape(1, -1),
        task_mix.T,
        task_diag.reshape(1, -1),
        task_noise.reshape(1, -1),
    )
    gathered = over_rows(share)
    own_y = [cols] + [
        lax.ppermute(cols, "row", [(i, (i + 2 * k) % n_row) for i in range(n_row)])
        for k in (1, 3, 2)
    ]
    other_y = [other_core(c) for c in own_y]
    stacked = jax.ShapeDtypeStruct((len(own_y),) + cols.shape, BF16)
    anywhere = pl.BlockSpec(memory_space=pl.ANY)
    pair_y = pl.pallas_call(
        functools.partial(stack_kernel, len(own_y)),
        in_specs=[VMEM] * len(own_y),
        out_specs=VMEM,
        out_shape=stacked,
        compiler_params=PARAMS,
        name="stack",
    )(*own_y)
    pair_y = lax.ppermute(pair_y, "col", [(i, i ^ 3) for i in range(n_col)])
    (sums,) = product_call(own_chunk, table, gathered, own_y + other_y)
    pair_y = pl.pallas_call(
        functools.partial(stack_kernel, 0),
        in_specs=[VMEM, anywhere],
        out_specs=VMEM,
        out_shape=stacked,
        compiler_params=PARAMS,
        name="gate",
    )(pair_y, sums)
    parts, own = product_call(own_chunk, table, gathered, [pair_y, other_core(pair_y)], (sums,))
    summed = over_rows(parts)
    send = pl.pallas_call(
        image_kernel,
        in_specs=[SMEM] + [VMEM] * 5,
        out_specs=VMEM,
        out_shape=jax.ShapeDtypeStruct((devices, 1, 384), F32),
        compiler_params=PARAMS,
        name="image",
    )(own_chunk, summed, own, vq, nv, pos)
    got = lax.all_to_all(send, ("row", "col"), split_axis=0, concat_axis=0, tiled=True)
    residual, direction, alpha, beta = pl.pallas_call(
        final_kernel,
        in_specs=[VMEM],
        out_specs=[VMEM] * 4,
        out_shape=[
            jax.ShapeDtypeStruct((width, rows), F32),
            jax.ShapeDtypeStruct((width, rows), F32),
            jax.ShapeDtypeStruct((1, width), F32),
            jax.ShapeDtypeStruct((1, width), F32),
        ],
        compiler_params=PARAMS,
        name="final",
    )(got)
    return residual.T, direction.T, alpha.reshape(width), beta.reshape(width)


def solution(mesh):
    axes = ("row", "col")
    return jax.shard_map(
        body,
        mesh=mesh,
        in_specs=(
            P(axes, None),
            P(axes),
            P(),
            P(axes),
            P(axes, None),
            P(),
            P(),
            P(),
            P(),
            P(),
            P(),
        ),
        out_specs=(P(axes, None), P(axes, None), P(), P()),
        check_vma=False,
    )
```

```python
import functools
import math

import jax
import jax.numpy as jnp
from jax import lax
from jax.experimental import pallas as pl
from jax.experimental.pallas import tpu as pltpu
from jax.sharding import PartitionSpec as P

F32 = jnp.float32
BF16 = jnp.bfloat16
VMEM = pl.BlockSpec(memory_space=pltpu.VMEM)
SMEM = pl.BlockSpec(memory_space=pltpu.SMEM)
PARAMS = pltpu.CompilerParams(vmem_limit_bytes=16 * 1024 * 1024)
ALONE = pltpu.CompilerParams(vmem_limit_bytes=60 * 1024 * 1024)
LARGE = pltpu.CompilerParams(vmem_limit_bytes=36 * 1024 * 1024)
V0, T0, N0, ONE, P0, S0, W0 = 64, 96, 97, 100, 103, 105, 112
LOG2E = math.log2(math.e)


def iota(shape, dim):
    return lax.broadcasted_iota(jnp.int32, shape, dim)


def split3(x):
    hi = x.astype(BF16)
    rest = x - hi.astype(F32)
    mid = rest.astype(BF16)
    low = (rest - mid.astype(F32)).astype(BF16)
    return hi, mid, low


def look_up(table, task):
    hit = (iota((table.shape[1], task.shape[1]), 0) == task).astype(BF16)
    tab = jnp.concatenate(split3(table), axis=0)
    got = jnp.dot(tab, hit, preferred_element_type=F32)
    return got[0:8] + got[8:16] + got[16:24]


def order_of(tid, cnt, rank):
    rows, ntask = tid.shape[1], cnt.shape[1]
    counts = cnt[...].astype(F32)
    before = iota((ntask, ntask), 1) < iota((ntask, ntask), 0)
    start = jnp.sum(jnp.where(before, counts, 0.0), axis=1, keepdims=True)
    hit = iota((ntask, rows), 0) == tid[...]
    pos = jnp.sum(jnp.where(hit, start, 0.0), axis=0, keepdims=True) + rank[...].astype(F32)
    pos_col = jnp.concatenate([pos, jnp.zeros((7, rows), F32)], axis=0).T[:, 0:1]
    return pos, jnp.sum((pos_col < pos).astype(F32), axis=0, keepdims=True)


def pack_kernel(
    feat, tid, cnt, rank, probes, net_w, net_b, scale, mix, diag, noise_in,
    cols, rows_out, vq_out, nv_out, pos_out, table_out, held,
):
    rows = feat.shape[1]
    width = probes.shape[0]
    pos, order = order_of(tid, cnt, rank)
    task = tid[...]
    table = jnp.concatenate(
        [mix[...], diag[...], noise_in[...], jnp.zeros((2, mix.shape[1]), F32)], axis=0
    )
    table_out[...] = table
    column = jnp.concatenate([net_b[...], scale[...], jnp.zeros((6, 64), F32)], axis=0).T
    hidden = jnp.tanh(
        lax.dot_general(
            net_w[...], feat[...], (((0,), (0,)), ((), ())), preferred_element_type=F32
        )
        + column[:, 0:1]
    )
    latent = (hidden * column[:, 1:2]).astype(BF16)
    lat = latent.astype(F32)
    norm = jnp.sum(lat * lat, axis=0, keepdims=True) * (-0.5 * LOG2E)
    local = pos - jnp.floor(pos * (1.0 / rows)) * rows
    high = jnp.floor(local * (1.0 / 16.0))
    found = look_up(table, task)
    extra = jnp.concatenate(
        [task.astype(F32)]
        + [a.astype(F32) for a in split3(norm)]
        + [jnp.ones((3, rows), F32), high, local - 16.0 * high]
        + [a.astype(F32) for a in split3(found[5:6])]
        + [jnp.zeros((4, rows), F32)]
        + [a.astype(F32) for a in split3(found[0:4])]
        + [jnp.zeros((4, rows), F32)],
        axis=0,
    ).astype(BF16)
    whole = jnp.concatenate([latent, probes[...], extra], axis=0)
    square = iota((rows, rows), 0)
    place_c = (square == order.astype(jnp.int32)).astype(BF16)
    turn = (((1,), (1,)), ((), ()))
    held[...] = lax.dot_general(place_c, whole, turn, preferred_element_type=F32)
    data = held[...].astype(BF16)
    cols[...] = data
    data = jnp.concatenate(
        [held[pl.ds(t + m, 16, stride=4), :] for t in range(0, rows, 64) for m in range(4)], axis=0
    )
    half = rows // 2
    pair = jnp.concatenate([data[:half, :V0], data[half:, :V0]], axis=1).astype(BF16)
    at = (iota((16, rows), 1) % 16 == iota((16, rows), 0)).astype(BF16)
    group = jnp.where(iota((rows, 128), 0) // 16 == iota((rows, 128), 1), data[:, T0 : T0 + 1], 0.0)
    tasks = jnp.dot(at, group.astype(BF16), preferred_element_type=F32).astype(BF16)
    for k in range(rows_out.shape[0]):
        rows_out[k, :half, :] = pair
        rows_out[k, half:, :] = tasks
    place = data[:, P0 : P0 + 1] * 16.0 + data[:, P0 + 1 : P0 + 2]
    noise_c = data[:, S0 : S0 + 1] + data[:, S0 + 1 : S0 + 2] + data[:, S0 + 2 : S0 + 3]
    v = data[:, V0:T0]
    nv = noise_c * v

    def fold(x, m):
        return jnp.concatenate(
            [x[t * 64 + m * 16 : t * 64 + m * 16 + 16] for t in range(rows // 64)], axis=0
        )

    vq_out[...] = jnp.concatenate([fold(v, m) for m in range(4)], axis=1)
    nv_out[...] = jnp.concatenate([fold(nv, m) for m in range(4)], axis=1)
    lane = iota((rows // 4, 128), 1)
    posq = jnp.zeros((rows // 4, 128), F32)
    for m in range(4):
        posq = jnp.where(lane == 3 * width + m, fold(place, m), posq)
    pos_out[...] = posq


def prepare_cols(cols, zc, st):
    chunks = []
    for c in cols:
        chunks += [c] if len(c.shape) == 2 else [c.at[h] for h in range(c.shape[0])]
    rows = chunks[0].shape[0]
    size = 4 * 16 * len(chunks)
    width = T0 - V0
    for k in range(rows // 64):
        data = jnp.concatenate(
            [c[g * 16 : g * 16 + 16, :] for g in range(4 * k, 4 * k + 4) for c in chunks],
            axis=0,
        )
        span = slice(k * size, (k + 1) * size)
        wide = data.astype(F32)
        zc[span, 128:] = data
        zc[span, :128] = jnp.where(iota((size, 128), 1) < V0, wide, pltpu.roll(wide, V0, 1)).astype(BF16)
        turned = wide.T
        weight = turned[W0 : W0 + 4] + turned[W0 + 4 : W0 + 8] + turned[W0 + 8 : W0 + 12]
        values = turned[V0:T0]
        for q in range(4):
            st[q * width : (q + 1) * width, span] = (weight[q : q + 1] * values).astype(BF16)
        st[4 * width :, span] = values.astype(BF16)


def product_kernel(tile, pieces, last, own_chunk, table, gathered, *refs):
    cols, refs = refs[:pieces], refs[pieces:]
    if last:
        before, out, own, kern_ref, task_ref, zc, st, mine = refs
    else:
        out, kern_ref, task_ref, zc, st = refs
    i = pl.program_id(0)
    steps = pl.num_programs(0)
    chunks = gathered.shape[0]
    half = gathered.shape[1] - 16
    tab = table[...]

    @pl.when(i == 0)
    def _():
        every = gathered[:, half:, :].reshape(chunks * 16, 128).astype(F32).T
        for k in range(task_ref.shape[0]):
            task_ref[k] = every[8 * k : 8 * k + 8]
        prepare_cols(cols, zc, st)

    first = pl.multiple_of(lax.rem(i, steps // 2) * 128, 128)
    blocks = [gathered[k, pl.ds(first, 128), :] for k in range(chunks)]
    data = jnp.concatenate(
        [b[g * 16 : g * 16 + 16, :] for g in range(8) for b in blocks], axis=0
    )
    rows = data.shape[0]
    turned = data.astype(F32).T
    z = jnp.where(i < steps // 2, turned[:V0], turned[V0:])
    norm = jnp.sum(z * z, axis=0, keepdims=True) * (-0.5 * LOG2E)
    parts = [a.astype(F32) for a in split3(norm)]
    sub = iota((T0 - V0, rows), 0)
    extra = jnp.where(jnp.logical_and(sub >= N0 - T0, sub < ONE - T0), 1.0, 0.0)
    for k in range(3):
        extra = jnp.where(sub == ONE - T0 + k, parts[k], extra)
    z = jnp.concatenate(
        split3(z * LOG2E) + (jnp.zeros((T0 - V0, rows), BF16), extra.astype(BF16)), axis=0
    )
    eight = task_ref[i]
    task = jnp.concatenate([eight[m : m + 1] for m in range(8)], axis=1)
    weight = look_up(tab, task.astype(jnp.int32))
    width = st.shape[0] // 5
    total = None
    for j in range(zc.shape[0] // tile):
        span = slice(j * tile, (j + 1) * tile)
        x = jnp.dot(zc[span, :], z, preferred_element_type=F32)
        kern = jnp.minimum(jnp.exp2(x).astype(BF16), jnp.asarray(1.0, BF16))
        kern_ref[span, :] = kern
        part = jnp.dot(st[: 4 * width, span], kern, preferred_element_type=F32)
        total = part if total is None else total + part
    low = weight[0:1] * total[:width]
    for q in range(1, 4):
        low = low + weight[q : q + 1] * total[q * width : (q + 1) * width]
    size = zc.shape[0] // 32
    count = rows // 2
    quarter = count // 4
    for k in range(2):
        lanes = slice(k * count, (k + 1) * count)
        start = pl.multiple_of(jnp.clip(4 * (2 * i + k) - 1, 0, 26) * size, size)
        band = pl.ds(start, 6 * size)
        same = zc[band, 128 + T0 : 129 + T0] == task[:, lanes].astype(BF16)
        kept = jnp.where(same, kern_ref[band, lanes], jnp.asarray(0.0, BF16))
        diag = jnp.dot(st[4 * width :, band], kept, preferred_element_type=F32)
        summed = low[:, lanes] + weight[4:5, lanes] * diag
        folded = jnp.concatenate(
            [summed[:, m * quarter : (m + 1) * quarter] for m in range(4)], axis=0
        ).T.reshape(chunks, 16, 128)
        span = slice(k * 16, k * 16 + 16)
        if last:
            folded = folded + before[:, span, :]
            mine[...] = folded
            own[span, :] = mine[own_chunk[0]]
        out[:, span, :] = folded.astype(out.dtype)


def product_call(own_chunk, table, gathered, cols, before=()):
    chunks, packed, _ = gathered.shape
    total = sum(c.size // 128 for c in cols)
    quarter = (packed - 16) // 2
    steps = quarter // 32
    rows = chunks * 128
    block = pl.BlockSpec((chunks, 32, 128), lambda i: (0, i, 0))
    out_specs, scratch = [block], []
    out_shape = [jax.ShapeDtypeStruct((chunks, quarter, 128), BF16 if before else F32)]
    if before:
        out_specs.append(pl.BlockSpec((32, 128), lambda i: (i, 0)))
        out_shape.append(jax.ShapeDtypeStruct((quarter, 128), F32))
        scratch.append(pltpu.VMEM((chunks, 16, 128), F32))
    return pl.pallas_call(
        functools.partial(product_kernel, 2048, len(cols), bool(before)),
        grid=(steps,),
        in_specs=[SMEM] + [VMEM] * (2 + len(cols)) + [block] * len(before),
        out_specs=out_specs,
        out_shape=out_shape,
        scratch_shapes=[
            pltpu.VMEM((total, rows), BF16),
            pltpu.VMEM((steps, 8, chunks * 16), F32),
            pltpu.VMEM((total, 256), BF16),
            pltpu.VMEM((5 * (T0 - V0), total), BF16),
        ]
        + scratch,
        compiler_params=LARGE,
        cost_estimate=pl.CostEstimate(
            flops=2 * steps * rows * total * 512, bytes_accessed=4 << 20, transcendentals=0
        ),
        name="product",
    )(own_chunk, table, gathered, *cols, *before)


def stack_kernel(count, *refs):
    if count == 0:
        refs[-1][...] = refs[0][...]
    for k in range(count):
        refs[-1][k] = refs[k][...]


def image_kernel(col, parts, own, vq, nv, pos, send):
    img = own[...] + nv[...]
    for k in range(parts.shape[0]):
        img = img + jnp.where(k == col[0], 0.0, parts[k].astype(F32))
    v = vq[...]

    def over(x):
        s = jnp.sum(x, axis=0, keepdims=True)
        return s[:, 0:32] + s[:, 32:64] + s[:, 64:96] + s[:, 96:128]

    vv, vi = over(v * v), over(v * img)
    ratio = jnp.where(vv > 0.0, vi / jnp.where(vv > 0.0, vv, 1.0), 0.0)
    rest = img - jnp.concatenate([ratio] * 4, axis=1) * v
    row = jnp.concatenate([vv, vi, over(rest * rest), jnp.zeros_like(vv)], axis=1)
    send[:, 0, :128] = img
    send[:, 0, 128:256] = v
    send[:, 0, 256:] = pos[...] + row


def final_kernel(got, residual, direction, alpha_out, beta_out):
    n = got.shape[0]
    rows = residual.shape[1]
    every = got[:, 0, 256:]
    turned = every.T

    def over(axis, pick):
        vv, vi, rr = (pick(k) for k in range(3))
        total_v = jnp.sum(vv, axis=axis, keepdims=True)
        total_i = jnp.sum(vi, axis=axis, keepdims=True)
        ratio = jnp.where(vv > 0.0, vi / jnp.where(vv > 0.0, vv, 1.0), 0.0)
        shift = ratio - total_i / total_v
        total_r = jnp.sum(rr + vv * (shift * shift), axis=axis, keepdims=True)
        alpha = total_v / total_i
        return alpha, alpha * alpha * total_r / total_v

    alpha, beta = over(1, lambda k: turned[32 * k : 32 * k + 32])
    sums = jnp.concatenate([alpha, beta, jnp.zeros((32, 126), F32)], axis=1).T
    alpha_out[...] = sums[0:1]
    beta_out[...] = sums[1:2]
    v = got[:, 0, 128:256].T
    res = v - jnp.concatenate([alpha] * 4, axis=0) * got[:, 0, :128].T
    pieces = split3(res) + (v.astype(BF16),)
    total = None
    for m in range(4):
        lanes = slice(m * 32, (m + 1) * 32)
        values = jnp.concatenate([p[lanes] for p in pieces], axis=0)
        place = every[:, 96 + m : 97 + m].astype(jnp.int32)
        onehot = (iota((n, rows), 1) == place).astype(BF16)
        part = jnp.dot(values, onehot, preferred_element_type=F32)
        total = part if total is None else total + part
    res_t = total[0:32] + total[32:64] + total[64:96]
    residual[...] = res_t
    direction[...] = res_t + beta * total[96:128]


def body(
    features,
    task_id,
    task_count,
    task_rank,
    probes,
    net_w,
    net_b,
    inv_scale,
    task_mix,
    task_diag,
    task_noise,
):
    rows = features.shape[0]
    n_row, n_col = lax.axis_size("row"), lax.axis_size("col")
    devices = n_row * n_col
    axes = ("row", "col")
    width = probes.shape[1]
    quarter = rows // 4
    col = lax.axis_index("col")
    own_chunk = (col // 4 * 2 + col % 2).astype(jnp.int32).reshape(1)
    groups = [[4 * x + z for x in range(n_col // 4) for z in pair] for pair in ((0, 1), (2, 3))]

    def over_rows(value):
        return lax.all_to_all(
            value, "col", split_axis=0, concat_axis=0, tiled=True, axis_index_groups=groups
        )

    def other_core(value):
        return lax.ppermute(value, "row", [(i, i ^ 1) for i in range(n_row)])

    shape = jax.ShapeDtypeStruct((quarter, 128), F32)
    cols, share, vq, nv, pos, table = pl.pallas_call(
        pack_kernel,
        in_specs=[VMEM] * 11,
        out_specs=[VMEM] * 6,
        out_shape=[
            jax.ShapeDtypeStruct((rows, 128), BF16),
            jax.ShapeDtypeStruct((n_col // 2, rows // 2 + 16, 128), BF16),
            shape,
            shape,
            shape,
            jax.ShapeDtypeStruct((8, task_count.shape[0]), F32),
        ],
        scratch_shapes=[pltpu.VMEM((rows, 128), F32)],
        compiler_params=ALONE,
        name="pack",
    )(
        features.T,
        task_id.reshape(1, -1),
        task_count.reshape(1, -1),
        task_rank.reshape(1, -1),
        probes.T,
        net_w,
        net_b.reshape(1, -1),
        inv_scale.reshape(1, -1),
        task_mix.T,
        task_diag.reshape(1, -1),
        task_noise.reshape(1, -1),
    )
    gathered = over_rows(share)
    own_y = [cols] + [
        lax.ppermute(cols, "row", [(i, (i + 2 * k) % n_row) for i in range(n_row)])
        for k in range(1, n_row // 2)
    ]
    other_y = [other_core(c) for c in own_y]
    stacked = jax.ShapeDtypeStruct((len(own_y),) + cols.shape, BF16)
    anywhere = pl.BlockSpec(memory_space=pl.ANY)
    pair_y = pl.pallas_call(
        functools.partial(stack_kernel, len(own_y)),
        in_specs=[VMEM] * len(own_y),
        out_specs=VMEM,
        out_shape=stacked,
        compiler_params=PARAMS,
        name="stack",
    )(*own_y)
    pair_y = lax.ppermute(pair_y, "col", [(i, i ^ 3) for i in range(n_col)])
    (sums,) = product_call(own_chunk, table, gathered, own_y + other_y)
    pair_y = pl.pallas_call(
        functools.partial(stack_kernel, 0),
        in_specs=[VMEM, anywhere],
        out_specs=VMEM,
        out_shape=stacked,
        compiler_params=PARAMS,
        name="gate",
    )(pair_y, sums)
    parts, own = product_call(own_chunk, table, gathered, [pair_y, other_core(pair_y)], (sums,))
    summed = over_rows(parts)
    send = pl.pallas_call(
        image_kernel,
        in_specs=[SMEM] + [VMEM] * 5,
        out_specs=VMEM,
        out_shape=jax.ShapeDtypeStruct((devices, 1, 384), F32),
        compiler_params=PARAMS,
        name="image",
    )(own_chunk, summed, own, vq, nv, pos)
    got = lax.all_to_all(send, ("row", "col"), split_axis=0, concat_axis=0, tiled=True)
    residual, direction, alpha, beta = pl.pallas_call(
        final_kernel,
        in_specs=[VMEM],
        out_specs=[VMEM] * 4,
        out_shape=[
            jax.ShapeDtypeStruct((width, rows), F32),
            jax.ShapeDtypeStruct((width, rows), F32),
            jax.ShapeDtypeStruct((1, width), F32),
            jax.ShapeDtypeStruct((1, width), F32),
        ],
        compiler_params=PARAMS,
        name="final",
    )(got)
    return residual.T, direction.T, alpha.reshape(width), beta.reshape(width)


def solution(mesh):
    axes = ("row", "col")
    return jax.shard_map(
        body,
        mesh=mesh,
        in_specs=(
            P(axes, None),
            P(axes),
            P(),
            P(axes),
            P(axes, None),
            P(),
            P(),
            P(),
            P(),
            P(),
            P(),
        ),
        out_specs=(P(axes, None), P(axes, None), P(), P()),
        check_vma=False,
    )
```
